1024 devices in a mesh: stream: 32 (over z_hi, y, core), trans: 32 (over x, z_lo).
Axes of the slice: x: 4, y: 8, z: 16 (z_hi: 2, z_lo: 8; z = z_hi * 8 + z_lo), core: 2. Of those that a mesh axis runs over, the one named last changes fastest.
Arguments:
- populations: float32 [19, 64, 256, 128], P(None, 'stream', 'trans'), may hold values from 0.01 to 0.2
- solid: int32 [64, 256, 128], P('stream', 'trans'), may hold values 0 or 1
- support: int32 [131072], P(('stream', 'trans')), may hold values from 0 to 32638, as said below
- fractions: float32 [3, 131072], P(None, ('stream', 'trans')), may hold values from 0 to 1
- target: float32 [3, 131072], P(None, ('stream', 'trans')), may hold values from -0.1 to 0.1
- area: float32 [131072], P(('stream', 'trans')), may hold values from 1 to 4
Outputs:
- new_populations: float32 [19, 64, 256, 128], P(None, 'stream', 'trans')
- marker_force: float32 [3, 131072], P(None, ('stream', 'trans'))
The draws below stay inside these ranges and needn't reach their ends.
Inputs may be any that keep to these rules, and one draw needn't show every extreme that they name: support[m] = (a * 256 + b) * 128 + e with a = 0 counted inside marker m's streamwise slab m // (128 * 32) (each cube spans the slab's two planes), 0 <= b <= 256 - 2 over the whole first transverse dimension and 0 <= e <= 126.
All inputs are finite; a program needn't handle non-finite values. No bound on the sum of `solid` on one device may be relied on, other than what follows from the above.
Results may differ from the reference program's by a relative error of at most 0.0003.
Values sent between devices are 32-bit elements; how exact they have to be, the bound alone decides.
A program may use at most 32 MiB of HBM per device.

```python
import math
import jax
import jax.numpy as jnp
from jax import lax

CX = 2
NZ = 128
MK = 128
STEPS = 2
NX = 64
NY = 256
MARKERS = 131072
N_TRANS = 32


def draw_support(key, part):
    subkeys = jax.random.split(key, 6)
    planes = jax.random.randint(subkeys[0], (MARKERS,), 0, CX - 1)
    depths = jax.random.randint(subkeys[1], (MARKERS,), 0, NZ - 1)
    spread_rows = jax.random.randint(subkeys[2], (MARKERS,), 0, NY - 1)
    centres = jax.random.randint(subkeys[3], (4,), 0, NY - 1)
    picker = jax.random.randint(subkeys[4], (MARKERS,), 0, 8)
    jitter = jax.random.randint(subkeys[5], (MARKERS,), -6, 7)
    folded = jnp.clip(centres[picker % 4] + jitter, 0, NY - 2)
    row_values = jnp.where(picker < 4, folded, spread_rows)
    cell_index = (planes * NY + row_values) * NZ + depths
    position = jnp.arange(MARKERS)
    cell_index = jnp.where(position == 0, 0, cell_index)
    cell_index = jnp.where(position == MARKERS - 1, (CX - 2) * NY * NZ + (NY - 2) * NZ + NZ - 2, cell_index)
    return cell_index.astype(jnp.int32)


def with_ends(entries, own_key, least, top_value):
    longest = entries.shape.index(max(entries.shape))
    spots = []
    for shift in (0, 1):
        where = [jax.random.randint(jax.random.fold_in(own_key, axis), (), 0, length) for axis, length in enumerate(entries.shape)]
        where[longest] = (where[longest] + shift) % entries.shape[longest]
        spots.append(tuple(where))
    return entries.at[spots[0]].set(least).at[spots[1]].set(top_value)


def block_scale(stream_key, dims, shards, low, top_value):
    loudness = 1.0
    for axis_at, shards_of in shards:
        draws = jax.random.uniform(jax.random.fold_in(jax.random.fold_in(stream_key, 6), axis_at), (shards_of,), jnp.float32, low / len(shards), top_value / len(shards))
        loudness = loudness * jnp.repeat(jnp.exp(draws), dims[axis_at] // shards_of).reshape((-1,) + (1,) * (len(dims) - 1 - axis_at))
    return loudness


def setup_inputs(seed: int = 0) -> dict:
    key_of = jax.random.split(jax.random.key(seed), 7)
    return {
        "populations": jnp.clip(0.01 + 0.19 * jax.random.uniform(key_of[0], (19, NX, NY, NZ), jnp.float32) ** block_scale(key_of[0], (19, NX, NY, NZ), ((1, 32), (2, 32)), -0.2, 0.2), 0.01, 0.2),
        "solid": with_ends((jax.random.randint(key_of[1], (NX, NY, NZ), 0, 8) < 1).astype(jnp.int32), jax.random.fold_in(key_of[1], 1), 0, 1),
        "support": draw_support(jax.random.fold_in(key_of[6], 71), 0),
        "fractions": jnp.clip(1.0 * jax.random.uniform(key_of[3], (3, MARKERS), jnp.float32) ** block_scale(key_of[3], (3, MARKERS), ((1, 1024),), -0.2, 0.2), 0.0, 1.0),
        "target": jnp.clip(jax.random.uniform(key_of[4], (3, MARKERS), jnp.float32, -0.1, 0.1) * block_scale(key_of[4], (3, MARKERS), ((1, 1024),), -0.4, 0.0), -0.1, 0.1),
        "area": jnp.clip(jnp.exp(math.log(4.0) - 1.3862944 * jax.random.uniform(key_of[5], (MARKERS,), jnp.float32) ** block_scale(key_of[5], (MARKERS,), ((0, 1024),), -0.2, 0.2)), 1.0, 4.0),
    }


velocity_table = ((0, 0, 0), (1, 0, 0), (-1, 0, 0), (0, 1, 0), (0, -1, 0), (0, 0, 1), (0, 0, -1), (1, 1, 0), (-1, -1, 0), (1, -1, 0), (-1, 1, 0), (1, 0, 1), (-1, 0, -1), (1, 0, -1), (-1, 0, 1), (0, 1, 1), (0, -1, -1), (0, 1, -1), (0, -1, 1))
weight_table = (1.0 / 3.0,) + (1.0 / 18.0,) * 6 + (1.0 / 36.0,) * 12
opposite = (0, 2, 1, 4, 3, 6, 5, 8, 7, 10, 9, 12, 11, 14, 13, 16, 15, 18, 17)
relax_base = 0.8
smagorinsky = 0.17

def signed_sum(factors, values):
    running = None
    for factor, value in zip(factors, values):
        if factor != 0:
            signed_term = value if factor > 0 else -value
            running = signed_term if running is None else running + signed_term
    return 0.0 if running is None else running

def moments(fields):
    density = fields[0]
    for member in range(1, 19):
        density = density + fields[member]
    momenta = []
    for dimension in range(3):
        momenta.append(signed_sum([velocity_table[member][dimension] for member in range(19)], [fields[member] for member in range(19)]))
    return (density, momenta)

def collide(fields, density, momenta, forcing, solid):
    velocity = [(momenta[dimension] + 0.5 * forcing[dimension]) / density for dimension in range(3)]
    square = velocity[0] * velocity[0] + velocity[1] * velocity[1] + velocity[2] * velocity[2]
    force_along = velocity[0] * forcing[0] + velocity[1] * forcing[1] + velocity[2] * forcing[2]
    projections = []
    nonequil = []
    for member in range(19):
        projected = signed_sum(velocity_table[member], velocity)
        equilibrium = weight_table[member] * density * (1.0 + 3.0 * projected + 4.5 * projected * projected - 1.5 * square)
        projections.append(projected)
        nonequil.append(fields[member] - equilibrium)
    magnitude_square = 0.0
    for first, second in ((0, 0), (1, 1), (2, 2), (0, 1), (0, 2), (1, 2)):
        component = signed_sum([velocity_table[member][first] * velocity_table[member][second] for member in range(19)], nonequil)
        factor = 1.0 if first == second else 2.0
        magnitude_square = magnitude_square + factor * component * component
    magnitude = jnp.sqrt(magnitude_square)
    relaxation = 0.5 * (relax_base + jnp.sqrt(relax_base * relax_base + 18.0 * math.sqrt(2.0) * smagorinsky * smagorinsky * magnitude / density))
    force_share = 1.0 - 0.5 / relaxation
    outputs = []
    for member in range(19):
        along_force = signed_sum(velocity_table[member], forcing)
        source = force_share * weight_table[member] * (3.0 * (along_force - force_along) + 9.0 * projections[member] * along_force)
        collided = fields[member] - nonequil[member] / relaxation + source
        outputs.append(jnp.where(solid == 1, fields[opposite[member]], collided))
    return jnp.stack(outputs)

def linear_share(fraction, offset):
    return fraction if offset else 1.0 - fraction

def reference(populations, solid, support, fractions, target, area):
    slab_index = jnp.arange(MARKERS, dtype=jnp.int32) // (MK * N_TRANS)
    depth_index = support % NZ
    remainder = support // NZ
    column = remainder % NY
    plane_index = remainder // NY + slab_index * CX
    corners = []
    for shift_x in (0, 1):
        for shift_y in (0, 1):
            for shift_z in (0, 1):
                flat_index = (((plane_index + shift_x) * NY + column + shift_y) * NZ + depth_index + shift_z).astype(jnp.int32)
                weight = linear_share(fractions[0], shift_x) * linear_share(fractions[1], shift_y) * linear_share(fractions[2], shift_z)
                corners.append((flat_index, weight))
    cell_count = NX * NY * NZ
    fields = populations
    force = jnp.zeros((3, MARKERS), jnp.float32)
    for repeat in range(STEPS):
        density, momenta = moments(fields)
        flat_velocity = jnp.stack([momenta[dimension] / density for dimension in range(3)]).reshape(3, cell_count)
        interpolated = jnp.zeros((3, MARKERS), jnp.float32)
        for flat_index, weight in corners:
            interpolated = interpolated + weight * flat_velocity[:, flat_index]
        force = area * (target - interpolated)
        forcing = jnp.zeros((3, cell_count), jnp.float32)
        for flat_index, weight in corners:
            forcing = forcing.at[:, flat_index].add(weight * force)
        forcing = forcing.reshape(3, NX, NY, NZ)
        momentum_stack = jnp.stack(momenta)

        def plane_update(position, fields=fields, density=density, momentum_stack=momentum_stack, forcing=forcing):
            plane_fields = lax.dynamic_index_in_dim(fields, position, 1, keepdims=False)
            plane_density = lax.dynamic_index_in_dim(density, position, 0, keepdims=False)
            plane_momenta = lax.dynamic_index_in_dim(momentum_stack, position, 1, keepdims=False)
            plane_forcing = lax.dynamic_index_in_dim(forcing, position, 1, keepdims=False)
            plane_solid = lax.dynamic_index_in_dim(solid, position, 0, keepdims=False)
            return collide(plane_fields, plane_density, [plane_momenta[0], plane_momenta[1], plane_momenta[2]], plane_forcing, plane_solid)
        collided_all = lax.map(plane_update, jnp.arange(NX, dtype=jnp.int32))
        passed = []
        for member in range(19):
            passed.append(jnp.roll(collided_all[:, member], velocity_table[member], axis=(0, 1, 2)))
        fields = jnp.stack(passed)
    return (fields, force)
```

```python
import functools
import math

import jax
import jax.numpy as jnp
from jax import lax
from jax.experimental import pallas as pl
from jax.experimental.pallas import tpu as pltpu
from jax.sharding import PartitionSpec as P

STEPS = 2
VEL = (
    (0, 0, 0),
    (1, 0, 0),
    (-1, 0, 0),
    (0, 1, 0),
    (0, -1, 0),
    (0, 0, 1),
    (0, 0, -1),
    (1, 1, 0),
    (-1, -1, 0),
    (1, -1, 0),
    (-1, 1, 0),
    (1, 0, 1),
    (-1, 0, -1),
    (1, 0, -1),
    (-1, 0, 1),
    (0, 1, 1),
    (0, -1, -1),
    (0, 1, -1),
    (0, -1, 1),
)
WEIGHT = (1.0 / 3.0,) + (1.0 / 18.0,) * 6 + (1.0 / 36.0,) * 12
OPP = (0, 2, 1, 4, 3, 6, 5, 8, 7, 10, 9, 12, 11, 14, 13, 16, 15, 18, 17)
TAU_BASE = 0.8
SMAG = 0.17
MESH = pl.DeviceIdType.MESH
UP = 0
DOWN = 1
GO_RIGHT = (1, 7, 9, 11, 13)
GO_LEFT = (2, 8, 10, 12, 14)
ROWS_UP = ((3, 0, 0), (3, 1, 1), (15, 0, 0), (15, 1, 1), (17, 0, 0), (17, 1, 1), (7, 0, 1), (10, 1, 0))
ROWS_DOWN = ((4, 0, 0), (4, 1, 1), (16, 0, 0), (16, 1, 1), (18, 0, 0), (18, 1, 1), (8, 1, 0), (9, 0, 1))


def add_up(terms):
    total = None
    for sign, value in terms:
        if sign == 0:
            continue
        if total is None:
            total = value if sign > 0 else -value
        else:
            total = total + value if sign > 0 else total - value
    return total


def combine(factors, values):
    total = add_up(zip(factors, values))
    return 0.0 if total is None else total


def moments(f):
    rho = add_up((1, f[i]) for i in range(19))
    mom = [add_up((VEL[i][d], f[i]) for i in range(19)) for d in range(3)]
    return rho, mom


def collide(f, rho, mom, g, solid):
    inv_rho = 1.0 / rho
    u = [(mom[d] + 0.5 * g[d]) * inv_rho for d in range(3)]
    square = u[0] * u[0] + u[1] * u[1] + u[2] * u[2]
    ug = u[0] * g[0] + u[1] * g[1] + u[2] * g[2]
    base = 1.0 - 1.5 * square
    proj = [combine(VEL[i], u) for i in range(19)]
    neq = []
    for i in range(19):
        feq = WEIGHT[i] * rho * (base + 3.0 * proj[i] + 4.5 * proj[i] * proj[i])
        neq.append(f[i] - feq)
    mag2 = 0.0
    for a, b in ((0, 0), (1, 1), (2, 2), (0, 1), (0, 2), (1, 2)):
        comp = combine([VEL[i][a] * VEL[i][b] for i in range(19)], neq)
        mag2 = mag2 + (1.0 if a == b else 2.0) * comp * comp
    mag = jnp.sqrt(mag2)
    tau = 0.5 * (
        TAU_BASE + jnp.sqrt(TAU_BASE * TAU_BASE + 18.0 * math.sqrt(2.0) * SMAG * SMAG * mag * inv_rho)
    )
    inv_tau = 1.0 / tau
    share = 1.0 - 0.5 * inv_tau
    is_solid = solid == 1
    out = []
    for i in range(19):
        cg = combine(VEL[i], g)
        source = share * (WEIGHT[i] * (3.0 * (cg - ug) + 9.0 * proj[i] * cg))
        out.append(jnp.where(is_solid, f[OPP[i]], f[i] - neq[i] * inv_tau + source))
    return out


def split(x):
    hi = x.astype(jnp.bfloat16)
    lo = (x - hi.astype(jnp.float32)).astype(jnp.bfloat16)
    return jnp.concatenate([hi, lo], axis=0)


def kernel(
    n_stream,
    n_trans,
    per_chunk,
    pop_ref,
    solid_ref,
    support_ref,
    frac_ref,
    target_ref,
    area_ref,
    out_ref,
    force_ref,
    gath,
    onehot,
    vs,
    gsum,
    htile,
    hrecv,
    hbuf,
    xsend,
    xrecv,
    ysend,
    yrecv,
    msend,
    mrecv,
    mown,
    dsend,
    drecv,
    uret,
    urecv,
    g_send,
    g_recv,
    h_send,
    h_recv,
    x_send,
    x_recv,
    y_send,
    y_recv,
    m_send,
    m_recv,
    d_send,
    d_recv,
    u_send,
    u_recv,
):
    s = lax.axis_index("stream")
    t = lax.axis_index("trans")
    s_next = lax.rem(s + 1, n_stream)
    s_prev = lax.rem(s + n_stream - 1, n_stream)
    t_next = lax.rem(t + 1, n_trans)
    t_prev = lax.rem(t + n_trans - 1, n_trans)
    diagonals = ((s_next, t_next), (s_prev, t_next), (s_next, t_prev), (s_prev, t_prev))

    barrier = pltpu.get_barrier_semaphore()

    def greet(k, carry):
        pl.semaphore_signal(
            barrier, inc=1, device_id=(s, lax.rem(t + k, n_trans)), device_id_type=MESH
        )
        return carry

    lax.fori_loop(1, n_trans, greet, 0)
    for where in ((s_next, t), (s_prev, t)) + diagonals:
        pl.semaphore_signal(barrier, inc=1, device_id=where, device_id_type=MESH)

    gath[0, 0:1, :] = support_ref[...].astype(jnp.float32)
    gath[0, 1:4, :] = frac_ref[...]
    gath[0, 4:7, :] = target_ref[...]
    gath[0, 7:8, :] = area_ref[...]

    f = [pop_ref[i] for i in range(19)]
    rho, mom = moments(f)
    inv = 1.0 / rho
    ustar = [mom[d] * inv for d in range(3)]
    htile[...] = jnp.zeros_like(htile)
    for p in range(2):
        for d in range(3):
            htile[UP, p * 4 + d : p * 4 + d + 1, :] = ustar[d][p, 7:8, :]
            htile[DOWN, p * 4 + d : p * 4 + d + 1, :] = ustar[d][p, 0:1, :]

    pl.semaphore_wait(barrier, n_trans - 1 + 6)

    def remote(src, dst, send, recv, where):
        return pltpu.make_async_remote_copy(
            src_ref=src, dst_ref=dst, send_sem=send, recv_sem=recv, device_id=where, device_id_type=MESH
        )

    copies = []

    def launch(*args):
        copy = remote(*args)
        copy.start()
        copies.append(copy)
        return copy

    halo = [
        launch(htile.at[UP], hrecv.at[UP], h_send.at[UP], h_recv.at[UP], (s, t_next)),
        launch(htile.at[DOWN], hrecv.at[DOWN], h_send.at[DOWN], h_recv.at[DOWN], (s, t_prev)),
    ]

    def gather_copy(k):
        return remote(
            gath.at[0], gath.at[k], g_send.at[k], g_recv.at[k], (s, lax.rem(t + k, n_trans))
        )

    def start_gather(k, carry):
        gather_copy(k).start()
        return carry

    lax.fori_loop(1, n_trans, start_gather, 0)

    for copy in halo:
        copy.wait_recv()

    hbuf[...] = jnp.zeros_like(hbuf)

    def set_halo(lo, hi):
        for p in range(2):
            hbuf[p, 0:3, :] = lo[p * 4 : p * 4 + 3, :]
            hbuf[p, 3:6, :] = hi[p * 4 : p * 4 + 3, :]

    def set_velocity(ustar):
        rows = []
        for shift in (0, 1):
            for d in range(3):
                for p in range(2):
                    x = ustar[d][p]
                    rows.append(pltpu.roll(x, 127, 1) if shift else x)
        for shift in (0, 1):
            for p in range(2):
                x = hbuf[p]
                rows.append(pltpu.roll(x, 127, 1) if shift else x)
        vs[...] = split(jnp.concatenate(rows, axis=0))

    set_halo(hrecv[UP], hrecv[DOWN])
    set_velocity(ustar)

    width = per_chunk * 128
    first_row = (t * 8).astype(jnp.float32)

    def marker_pass(step):
        gsum[...] = jnp.zeros_like(gsum)

        def chunk(j, carry):
            tile = jnp.concatenate([gath[j * per_chunk + i] for i in range(per_chunk)], axis=1)
            fx, fy, fz = tile[1:2], tile[2:3], tile[3:4]
            b = jnp.floor(tile[0:1] * (1.0 / 128.0))
            if step == 0:
                e = tile[0:1] - 128.0 * b
                depth = lax.broadcasted_iota(jnp.int32, (128, width), 0).astype(jnp.float32)
                pick = jnp.where(depth == e, 1.0, 0.0).astype(jnp.bfloat16)
                onehot[j] = pick
            else:
                pick = onehot[j]
            r = lax.dot_general(
                vs[...], pick, (((1,), (0,)), ((), ())), preferred_element_type=jnp.float32
            )
            r = r[0:128] + r[128:256]
            gx, gy, gz = 1.0 - fx, 1.0 - fy, 1.0 - fz
            local = lax.broadcasted_iota(jnp.int32, (8, width), 0).astype(jnp.float32)
            rel = b - first_row
            wy = jnp.where(local == rel, gy, 0.0) + jnp.where(local == rel + 1.0, fy, 0.0)
            wh = jnp.where(
                local < 3.0, jnp.where(rel == -1.0, gy, 0.0), jnp.where(rel == 7.0, fy, 0.0)
            )

            def lerp(at):
                planes = []
                for p in range(2):
                    low, high = at(0, p), at(1, p)
                    planes.append(low * gz + high * fz)
                return planes[0] * gx + planes[1] * fx

            edge = wh * lerp(lambda shift, p: r[(12 + shift * 2 + p) * 8 : (12 + shift * 2 + p) * 8 + 8])
            vel = []
            for d in range(3):
                own = lerp(
                    lambda shift, p: r[((shift * 3 + d) * 2 + p) * 8 : ((shift * 3 + d) * 2 + p) * 8 + 8]
                )
                vel.append(
                    jnp.sum(wy * own, axis=0, keepdims=True) + edge[d : d + 1] + edge[3 + d : 4 + d]
                )
            if step == STEPS - 1:
                mine = (rel >= 0.0) & (rel <= 7.0)
                for d in range(3):
                    back = jnp.where(mine, vel[d], 0.0)
                    for i in range(per_chunk):
                        uret[j * per_chunk + i, d : d + 1, :] = back[:, i * 128 : i * 128 + 128]
            spread = []
            wyz = [wy * gz, wy * fz]
            wx = (gx, fx)
            pushes = [tile[7:8] * (tile[4 + d : 5 + d] - vel[d]) for d in range(3)]
            for shift in (0, 1):
                for d in range(3):
                    for p in range(2):
                        spread.append(wyz[shift] * (pushes[d] * wx[p]))
            gsum[...] += lax.dot_general(
                split(jnp.concatenate(spread, axis=0)),
                pick,
                (((1,), (1,)), ((), ())),
                preferred_element_type=jnp.float32,
            )
            return carry

        lax.fori_loop(0, n_trans // per_chunk, chunk, 0)
        total = gsum[0:96] + gsum[96:192]
        g = []
        for d in range(3):
            planes = []
            for p in range(2):
                low = total[(d * 2 + p) * 8 : (d * 2 + p) * 8 + 8]
                high = total[((3 + d) * 2 + p) * 8 : ((3 + d) * 2 + p) * 8 + 8]
                planes.append(low + pltpu.roll(high, 1, 1))
            g.append(jnp.stack(planes))
        return g

    def wait_gather(k, carry):
        gather_copy(k).wait_recv()
        return carry

    lax.fori_loop(1, n_trans, wait_gather, 0)

    row_of = lax.broadcasted_iota(jnp.int32, (8, 128), 0)

    def deep(post):
        return [
            [
                pltpu.roll(post[i][p], VEL[i][2] % 128, 1) if VEL[i][2] else post[i][p]
                for p in range(2)
            ]
            for i in range(19)
        ]

    def exchange(step, moved):
        sent = []
        for q, i in enumerate(GO_RIGHT):
            xsend[step, 0, q] = moved[i][1]
        for q, i in enumerate(GO_LEFT):
            xsend[step, 1, q] = moved[i][0]
        sent.append(launch(xsend.at[step, 0], xrecv.at[step, 0], x_send.at[step, 0], x_recv.at[step, 0], (s_next, t)))
        sent.append(launch(xsend.at[step, 1], xrecv.at[step, 1], x_send.at[step, 1], x_recv.at[step, 1], (s_prev, t)))
        for q, (i, source, unused) in enumerate(ROWS_UP):
            ysend[step, UP, q : q + 1, :] = moved[i][source][7:8]
        for q, (i, source, unused) in enumerate(ROWS_DOWN):
            ysend[step, DOWN, q : q + 1, :] = moved[i][source][0:1]
        sent.append(launch(ysend.at[step, UP], yrecv.at[step, UP], y_send.at[step, UP], y_recv.at[step, UP], (s, t_next)))
        sent.append(launch(ysend.at[step, DOWN], yrecv.at[step, DOWN], y_send.at[step, DOWN], y_recv.at[step, DOWN], (s, t_prev)))
        corner = ((7, 1, 7), (10, 0, 7), (9, 1, 0), (8, 0, 0))
        for q, (i, source, row) in enumerate(corner):
            dsend[step, q] = jnp.broadcast_to(moved[i][source][row : row + 1], (8, 128))
        if step < STEPS - 1:
            for side, sign, row in ((UP, 1, 7), (DOWN, -1, 0)):
                inner = row - sign
                for p in range(2):
                    level = {0: [], sign: []}
                    own = []
                    for i in range(19):
                        source = p - VEL[i][0]
                        if source not in (0, 1):
                            continue
                        if VEL[i][1] in level:
                            level[VEL[i][1]].append((i, moved[i][source]))
                        else:
                            own.append((i, moved[i][source]))
                    for m in range(4):
                        flat = sum_moment(level[0], m)
                        steep = sum_moment(level[sign], m)
                        value = 0.0
                        if flat is not None:
                            value = flat[row : row + 1]
                        if steep is not None:
                            value = value + steep[inner : inner + 1]
                        msend[side, p * 4 + m : p * 4 + m + 1, :] = value
                        mine = sum_moment(own, m)
                        mown[side, p * 4 + m : p * 4 + m + 1, :] = (
                            jnp.zeros((1, 128), jnp.float32) if mine is None else mine[7 - row : 8 - row]
                        )
                for q, names, source, at in ((0, GO_RIGHT, 1, 0), (1, GO_LEFT, 0, 4)):
                    q = q + (0 if side == UP else 2)
                    flat_set = [(i, moved[i][source]) for i in names if VEL[i][1] == 0]
                    steep_set = [(i, moved[i][source]) for i in names if VEL[i][1] == sign]
                    for m in range(4):
                        flat = sum_moment(flat_set, m)
                        steep = sum_moment(steep_set, m)
                        value = 0.0
                        if flat is not None:
                            value = flat[row : row + 1]
                        if steep is not None:
                            value = value + steep[inner : inner + 1]
                        dsend[step, q, at + m : at + m + 1, :] = value
            sent.append(launch(msend.at[UP], mrecv.at[UP], m_send.at[UP], m_recv.at[UP], (s, t_next)))
            sent.append(launch(msend.at[DOWN], mrecv.at[DOWN], m_send.at[DOWN], m_recv.at[DOWN], (s, t_prev)))
        for q, where in enumerate(diagonals):
            sent.append(launch(dsend.at[step, q], drecv.at[step, q], d_send.at[step, q], d_recv.at[step, q], where))
        return sent

    def sum_moment(members, m):
        if m == 0:
            return add_up((1, value) for i, value in members)
        return add_up((VEL[i][m - 1], value) for i, value in members)

    def stream(step, moved):
        new = []
        for i in range(19):
            cx, cy, unused = VEL[i]
            planes = []
            for p in range(2):
                source = p - cx
                if source in (0, 1):
                    tile = moved[i][source]
                elif cx == 1:
                    tile = xrecv[step, 0, GO_RIGHT.index(i)]
                else:
                    tile = xrecv[step, 1, GO_LEFT.index(i)]
                if cy != 0:
                    side = UP if cy == 1 else DOWN
                    rows = ROWS_UP if cy == 1 else ROWS_DOWN
                    if source in (0, 1):
                        at = rows.index((i, source, p))
                        edge = yrecv[step, side, at : at + 1, :]
                    else:
                        q = (0 if cx == 1 else 1) + (0 if cy == 1 else 2)
                        at = 4 if cx == 1 else 0
                        edge = drecv[step, q, at : at + 1, :]
                    tile = jnp.where(row_of == (0 if cy == 1 else 7), edge, pltpu.roll(tile, cy % 8, 0))
                planes.append(tile)
            new.append(jnp.stack(planes))
        return new

    def edge_moments(step, side):
        low = row_of < 4
        total = mrecv[side] + mown[side]
        q = 0 if side == UP else 2
        total = total + jnp.where(low, drecv[step, q], drecv[step, q + 1])
        sign = 1 if side == UP else -1
        row = 0 if side == UP else 7
        i = 9 if side == UP else 7
        left = xrecv[step, 0, GO_RIGHT.index(i), row : row + 1, :]
        i = 8 if side == UP else 10
        right = xrecv[step, 1, GO_LEFT.index(i), row : row + 1, :]
        total = total + jnp.where((row_of == 0) | (row_of == 1), left, 0.0)
        total = total + jnp.where(row_of == 2, -sign * left, 0.0)
        total = total + jnp.where(row_of == 4, right, 0.0)
        total = total + jnp.where(row_of == 5, -right, 0.0)
        total = total + jnp.where(row_of == 6, -sign * right, 0.0)
        return total

    def edge_velocity(total):
        values = []
        for p in range(2):
            inv = 1.0 / total[p * 4 : p * 4 + 1]
            values.append(total[p * 4 + 1 : p * 4 + 4] * inv)
        return values

    solid = solid_ref[...]

    g = marker_pass(0)
    moved = deep(collide(f, rho, mom, g, solid))
    for copy in exchange(0, moved):
        copy.wait_recv()
    f = stream(0, moved)
    low = edge_velocity(edge_moments(0, UP))
    high = edge_velocity(edge_moments(0, DOWN))
    for p in range(2):
        hbuf[p, 0:3, :] = low[p]
        hbuf[p, 3:6, :] = high[p]
    rho, mom = moments(f)
    inv = 1.0 / rho
    set_velocity([mom[d] * inv for d in range(3)])

    g = marker_pass(1)

    def return_copy(k):
        return remote(
            uret.at[k],
            urecv.at[k],
            u_send.at[k],
            u_recv.at[k],
            (s, lax.rem(t + n_trans - k, n_trans)),
        )

    def start_return(k, carry):
        return_copy(k).start()
        return carry

    lax.fori_loop(1, n_trans, start_return, 0)
    moved = deep(collide(f, rho, mom, g, solid))
    for copy in exchange(1, moved):
        copy.wait_recv()
    f = stream(1, moved)
    for i in range(19):
        out_ref[i] = f[i]

    def wait_return(k, carry):
        return_copy(k).wait_recv()
        return carry

    lax.fori_loop(1, n_trans, wait_return, 0)
    vel = uret[0]
    for k in range(1, n_trans):
        vel = vel + urecv[k]
    force_ref[...] = gath[0, 7:8, :] * (gath[0, 4:7, :] - vel[0:3])

    for copy in copies:
        copy.wait_send()

    def wait_sends(k, carry):
        gather_copy(k).wait_send()
        return_copy(k).wait_send()
        return carry

    lax.fori_loop(1, n_trans, wait_sends, 0)


def per_device(n_stream, n_trans, populations, solid, support, fractions, target, area):
    per_chunk = math.gcd(n_trans, 8)
    dma = pltpu.SemaphoreType.DMA
    f32 = jnp.float32
    vmem = pl.BlockSpec(memory_space=pltpu.VMEM)
    markers = support.shape[0]
    return pl.pallas_call(
        functools.partial(kernel, n_stream, n_trans, per_chunk),
        out_shape=(
            jax.ShapeDtypeStruct(populations.shape, f32),
            jax.ShapeDtypeStruct((3, markers), f32),
        ),
        in_specs=[vmem] * 6,
        out_specs=(vmem, vmem),
        scratch_shapes=[
            pltpu.VMEM((n_trans, 8, 128), f32),
            pltpu.VMEM((n_trans // per_chunk, 128, per_chunk * 128), jnp.bfloat16),
            pltpu.VMEM((256, 128), jnp.bfloat16),
            pltpu.VMEM((192, 128), f32),
            pltpu.VMEM((2, 8, 128), f32),
            pltpu.VMEM((2, 8, 128), f32),
            pltpu.VMEM((2, 8, 128), f32),
            pltpu.VMEM((2, 2, 5, 8, 128), f32),
            pltpu.VMEM((2, 2, 5, 8, 128), f32),
            pltpu.VMEM((2, 2, 8, 128), f32),
            pltpu.VMEM((2, 2, 8, 128), f32),
            pltpu.VMEM((2, 8, 128), f32),
            pltpu.VMEM((2, 8, 128), f32),
            pltpu.VMEM((2, 8, 128), f32),
            pltpu.VMEM((2, 4, 8, 128), f32),
            pltpu.VMEM((2, 4, 8, 128), f32),
            pltpu.VMEM((n_trans, 3, 128), f32),
            pltpu.VMEM((n_trans, 3, 128), f32),
            dma((n_trans,)),
            dma((n_trans,)),
            dma((2,)),
            dma((2,)),
            dma((2, 2)),
            dma((2, 2)),
            dma((2, 2)),
            dma((2, 2)),
            dma((2,)),
            dma((2,)),
            dma((2, 4)),
            dma((2, 4)),
            dma((n_trans,)),
            dma((n_trans,)),
        ],
        compiler_params=pltpu.CompilerParams(
            collective_id=0, has_side_effects=True, vmem_limit_bytes=40 * 1024 * 1024
        ),
        name="tract",
    )(
        populations,
        solid,
        support.reshape(1, markers),
        fractions,
        target,
        area.reshape(1, markers),
    )


def solution(mesh):
    placed = (
        P(None, "stream", "trans", None),
        P("stream", "trans", None),
        P(("stream", "trans")),
        P(None, ("stream", "trans")),
        P(None, ("stream", "trans")),
        P(("stream", "trans")),
    )
    return jax.shard_map(
        functools.partial(per_device, mesh.shape["stream"], mesh.shape["trans"]),
        mesh=mesh,
        in_specs=placed,
        out_specs=(P(None, "stream", "trans", None), P(None, ("stream", "trans"))),
        check_vma=False,
    )
```

```python
import functools
import math

import jax
import jax.numpy as jnp
from jax import lax
from jax.experimental import pallas as pl
from jax.experimental.pallas import tpu as pltpu
from jax.sharding import PartitionSpec as P

STEPS = 2
VEL = (
    (0, 0, 0),
    (1, 0, 0),
    (-1, 0, 0),
    (0, 1, 0),
    (0, -1, 0),
    (0, 0, 1),
    (0, 0, -1),
    (1, 1, 0),
    (-1, -1, 0),
    (1, -1, 0),
    (-1, 1, 0),
    (1, 0, 1),
    (-1, 0, -1),
    (1, 0, -1),
    (-1, 0, 1),
    (0, 1, 1),
    (0, -1, -1),
    (0, 1, -1),
    (0, -1, 1),
)
WEIGHT = (1.0 / 3.0,) + (1.0 / 18.0,) * 6 + (1.0 / 36.0,) * 12
OPP = (0, 2, 1, 4, 3, 6, 5, 8, 7, 10, 9, 12, 11, 14, 13, 16, 15, 18, 17)
TAU_BASE = 0.8
SMAG = 0.17
MESH = pl.DeviceIdType.MESH
UP = 0
DOWN = 1
GO_RIGHT = (1, 7, 9, 11, 13)
GO_LEFT = (2, 8, 10, 12, 14)
ROWS_UP = ((3, 0, 0), (3, 1, 1), (15, 0, 0), (15, 1, 1), (17, 0, 0), (17, 1, 1), (7, 0, 1), (10, 1, 0))
ROWS_DOWN = ((4, 0, 0), (4, 1, 1), (16, 0, 0), (16, 1, 1), (18, 0, 0), (18, 1, 1), (8, 1, 0), (9, 0, 1))


def add_up(terms):
    total = None
    for sign, value in terms:
        if sign == 0:
            continue
        if total is None:
            total = value if sign > 0 else -value
        else:
            total = total + value if sign > 0 else total - value
    return total


def combine(factors, values):
    total = add_up(zip(factors, values))
    return 0.0 if total is None else total


def moments(f):
    rho = add_up((1, f[i]) for i in range(19))
    mom = [add_up((VEL[i][d], f[i]) for i in range(19)) for d in range(3)]
    return rho, mom


def collide(f, rho, mom, g, solid):
    inv_rho = 1.0 / rho
    u = [(mom[d] + 0.5 * g[d]) * inv_rho for d in range(3)]
    square = u[0] * u[0] + u[1] * u[1] + u[2] * u[2]
    ug = u[0] * g[0] + u[1] * g[1] + u[2] * g[2]
    base = 1.0 - 1.5 * square
    proj = [combine(VEL[i], u) for i in range(19)]
    neq = []
    for i in range(19):
        feq = WEIGHT[i] * rho * (base + 3.0 * proj[i] + 4.5 * proj[i] * proj[i])
        neq.append(f[i] - feq)
    mag2 = 0.0
    for a, b in ((0, 0), (1, 1), (2, 2), (0, 1), (0, 2), (1, 2)):
        comp = combine([VEL[i][a] * VEL[i][b] for i in range(19)], neq)
        mag2 = mag2 + (1.0 if a == b else 2.0) * comp * comp
    mag = jnp.sqrt(mag2)
    tau = 0.5 * (
        TAU_BASE + jnp.sqrt(TAU_BASE * TAU_BASE + 18.0 * math.sqrt(2.0) * SMAG * SMAG * mag * inv_rho)
    )
    inv_tau = 1.0 / tau
    share = 1.0 - 0.5 * inv_tau
    is_solid = solid == 1
    out = []
    for i in range(19):
        cg = combine(VEL[i], g)
        source = share * (WEIGHT[i] * (3.0 * (cg - ug) + 9.0 * proj[i] * cg))
        out.append(jnp.where(is_solid, f[OPP[i]], f[i] - neq[i] * inv_tau + source))
    return out


def split(x, axis):
    hi = x.astype(jnp.bfloat16)
    lo = (x - hi.astype(jnp.float32)).astype(jnp.bfloat16)
    return jnp.concatenate([hi, lo], axis=axis)


def kernel(
    n_stream,
    n_trans,
    columns,
    pop_hbm,
    solid_hbm,
    support_hbm,
    frac_hbm,
    target_hbm,
    area_hbm,
    out_ref,
    force_ref,
    pop_ref,
    solid_ref,
    support_ref,
    frac_ref,
    target_ref,
    area_ref,
    gath,
    onehot,
    vs,
    htile,
    hrecv,
    hbuf,
    xsend,
    xrecv,
    ysend,
    yrecv,
    ylast,
    ylast_recv,
    mown,
    dsend,
    drecv,
    uret,
    urecv,
    in_sem,
    g_send,
    g_recv,
    h_send,
    h_recv,
    x_send,
    x_recv,
    y_send,
    y_recv,
    d_send,
    d_recv,
    u_send,
    u_recv,
):
    s = lax.axis_index("stream")
    t = lax.axis_index("trans")
    s_next = lax.rem(s + 1, n_stream)
    s_prev = lax.rem(s + n_stream - 1, n_stream)
    t_next = lax.rem(t + 1, n_trans)
    t_prev = lax.rem(t + n_trans - 1, n_trans)
    diagonals = ((s_next, t_next), (s_prev, t_next), (s_next, t_prev), (s_prev, t_prev))

    run = n_trans // columns
    x = t // run
    z = lax.rem(t, run)
    upper = (2 * z) // run
    far_first = [upper * q + (1 - upper) * (run - 1 - q) for q in range(run)]
    far_columns = (2, 1, 3) if columns == 4 else tuple(range(1, columns))

    def column(offset):
        return lax.rem(x + offset, columns)

    loads = [
        pltpu.make_async_copy(source, target, in_sem.at[k])
        for k, (source, target) in enumerate(
            (
                (pop_hbm, pop_ref),
                (support_hbm, support_ref),
                (frac_hbm, frac_ref),
                (target_hbm, target_ref),
                (area_hbm, area_ref),
                (solid_hbm, solid_ref),
            )
        )
    ]
    barrier = pltpu.get_barrier_semaphore()

    def greet(where):
        pl.semaphore_signal(barrier, inc=1, device_id=where, device_id_type=MESH)

    for where in diagonals + ((s_next, t), (s_prev, t)):
        greet(where)
    for offset in far_columns:
        for row in far_first:
            greet((s, column(offset) * run + row))
    for row in far_first:
        pl.when(row != z)(functools.partial(greet, (s, x * run + row)))
    for load in loads:
        load.start()
    for load in loads:
        load.wait()

    gath[t, 0:1, :] = support_ref[...].astype(jnp.float32)
    gath[t, 1:4, :] = frac_ref[...]
    gath[t, 4:7, :] = target_ref[...]
    gath[t, 7:8, :] = area_ref[...]

    f = [pop_ref[i] for i in range(19)]
    rho, mom = moments(f)
    inv = 1.0 / rho
    ustar = [mom[d] * inv for d in range(3)]
    htile[...] = jnp.zeros_like(htile)
    for p in range(2):
        for d in range(3):
            htile[UP, p * 4 + d : p * 4 + d + 1, :] = ustar[d][p, 7:8, :]
            htile[DOWN, p * 4 + d : p * 4 + d + 1, :] = ustar[d][p, 0:1, :]

    pl.semaphore_wait(barrier, n_trans - 1 + 6)

    def remote(src, dst, send, recv, where):
        return pltpu.make_async_remote_copy(
            src_ref=src, dst_ref=dst, send_sem=send, recv_sem=recv, device_id=where, device_id_type=MESH
        )

    copies = []

    def launch(*args):
        copy = remote(*args)
        copy.start()
        copies.append(copy)
        return copy

    halo = [
        launch(htile.at[UP], hrecv.at[UP], h_send.at[UP], h_recv.at[UP], (s, t_next)),
        launch(htile.at[DOWN], hrecv.at[DOWN], h_send.at[DOWN], h_recv.at[DOWN], (s, t_prev)),
    ]

    def gather_copy(k):
        return remote(gath.at[t], gath.at[t], g_send.at[k], g_recv.at[t], (s, k))

    def gather_wait(k):
        remote(gath.at[t], gath.at[k], g_send.at[k], g_recv.at[k], (s, k)).wait_recv()

    for offset in far_columns:
        for row in far_first:
            gather_copy(column(offset) * run + row).start()
    for row in far_first:
        pl.when(row != z)(lambda row=row: gather_copy(x * run + row).start())

    for copy in halo:
        copy.wait_recv()

    hbuf[...] = jnp.zeros_like(hbuf)

    def set_halo(lo, hi):
        for p in range(2):
            hbuf[p, 0:3, :] = lo[p * 4 : p * 4 + 3, :]
            hbuf[p, 3:6, :] = hi[p * 4 : p * 4 + 3, :]

    def set_velocity(ustar):
        rows = []
        for shift in (0, 1):
            for d in range(3):
                for p in range(2):
                    x = ustar[d][p]
                    rows.append(pltpu.roll(x, 127, 1) if shift else x)
        for shift in (0, 1):
            for p in range(2):
                x = hbuf[p]
                rows.append(pltpu.roll(x, 127, 1) if shift else x)
        vs[...] = split(jnp.concatenate(rows, axis=0), 1)

    set_halo(hrecv[UP], hrecv[DOWN])
    set_velocity(ustar)

    width = run * 128
    first_row = (t * 8).astype(jnp.float32)

    def return_copy(k):
        return remote(uret.at[k], urecv.at[t], u_send.at[k], u_recv.at[t], (s, k))

    def return_wait(k):
        remote(uret.at[k], urecv.at[k], u_send.at[k], u_recv.at[k], (s, k)).wait_recv()

    def marker_pass(step):
        def chunk(j):
            first = column(j) * run
            if step == 0:
                for i in range(run):
                    if j:
                        gather_wait(first + i)
                    else:
                        pl.when(z != i)(functools.partial(gather_wait, first + i))
            tile = jnp.concatenate([gath[first + i] for i in range(run)], axis=1)
            fx, fy, fz = tile[1:2], tile[2:3], tile[3:4]
            b = jnp.floor(tile[0:1] * (1.0 / 128.0))
            if step == 0:
                e = tile[0:1] - 128.0 * b
                depth = lax.broadcasted_iota(jnp.int32, (128, width), 0).astype(jnp.float32)
                pick = jnp.where(depth == e, 1.0, 0.0).astype(jnp.bfloat16)
                onehot[j] = pick
            else:
                pick = onehot[j]
            r = lax.dot_general(
                vs[...],
                jnp.concatenate([pick, pick], axis=0),
                (((1,), (0,)), ((), ())),
                preferred_element_type=jnp.float32,
            )
            gx, gy, gz = 1.0 - fx, 1.0 - fy, 1.0 - fz
            local = lax.broadcasted_iota(jnp.int32, (8, width), 0).astype(jnp.float32)
            rel = b - first_row
            wy = jnp.where(local == rel, gy, 0.0) + jnp.where(local == rel + 1.0, fy, 0.0)
            wh = jnp.where(
                local < 3.0, jnp.where(rel == -1.0, gy, 0.0), jnp.where(rel == 7.0, fy, 0.0)
            )

            def lerp(at):
                planes = []
                for p in range(2):
                    low, high = at(0, p), at(1, p)
                    planes.append(low * gz + high * fz)
                return planes[0] * gx + planes[1] * fx

            edge = wh * lerp(lambda shift, p: r[(12 + shift * 2 + p) * 8 : (12 + shift * 2 + p) * 8 + 8])
            vel = []
            for d in range(3):
                own = lerp(
                    lambda shift, p: r[((shift * 3 + d) * 2 + p) * 8 : ((shift * 3 + d) * 2 + p) * 8 + 8]
                )
                vel.append(
                    jnp.sum(wy * own, axis=0, keepdims=True) + edge[d : d + 1] + edge[3 + d : 4 + d]
                )
            if step == STEPS - 1:
                mine = (rel >= 0.0) & (rel <= 7.0)
                for d in range(3):
                    back = jnp.where(mine, vel[d], 0.0)
                    for i in range(run):
                        uret[first + i, d : d + 1, :] = back[:, i * 128 : i * 128 + 128]
                for i in range(run):
                    if j:
                        return_copy(first + i).start()
                    else:
                        pl.when(z != i)(lambda i=i: return_copy(first + i).start())
            spread = []
            wyz = [wy * gz, wy * fz]
            wx = (gx, fx)
            pushes = [tile[7:8] * (tile[4 + d : 5 + d] - vel[d]) for d in range(3)]
            for shift in (0, 1):
                for d in range(3):
                    for p in range(2):
                        spread.append(wyz[shift] * (pushes[d] * wx[p]))
            return lax.dot_general(
                split(jnp.concatenate(spread, axis=0), 0),
                pick,
                (((1,), (1,)), ((), ())),
                preferred_element_type=jnp.float32,
            )

        order = (0,) + far_columns[::-1] if step == 0 else far_columns + (0,)
        total = None
        for j in order:
            part = chunk(j)
            total = part if total is None else total + part
        total = total[0:96] + total[96:192]
        g = []
        for d in range(3):
            planes = []
            for p in range(2):
                low = total[(d * 2 + p) * 8 : (d * 2 + p) * 8 + 8]
                high = total[((3 + d) * 2 + p) * 8 : ((3 + d) * 2 + p) * 8 + 8]
                planes.append(low + pltpu.roll(high, 1, 1))
            g.append(jnp.stack(planes))
        return g

    row_of = lax.broadcasted_iota(jnp.int32, (8, 128), 0)

    def deep(post):
        return [
            [
                pltpu.roll(post[i][p], VEL[i][2] % 128, 1) if VEL[i][2] else post[i][p]
                for p in range(2)
            ]
            for i in range(19)
        ]

    def put_row(step, side, at, value):
        if step < STEPS - 1:
            ysend[side, 0, at : at + 1, :] = value
        else:
            ylast[side, at : at + 1, :] = value

    def got_row(step, side, at):
        if step < STEPS - 1:
            return yrecv[side, 0, at : at + 1, :]
        return ylast_recv[side, at : at + 1, :]

    def exchange(step, moved):
        sent = []
        for q, i in enumerate(GO_RIGHT):
            xsend[step, 0, q] = moved[i][1]
        for q, i in enumerate(GO_LEFT):
            xsend[step, 1, q] = moved[i][0]
        sent.append(launch(xsend.at[step, 0], xrecv.at[step, 0], x_send.at[step, 0], x_recv.at[step, 0], (s_next, t)))
        sent.append(launch(xsend.at[step, 1], xrecv.at[step, 1], x_send.at[step, 1], x_recv.at[step, 1], (s_prev, t)))
        for q, (i, source, unused) in enumerate(ROWS_UP):
            put_row(step, UP, q, moved[i][source][7:8])
        for q, (i, source, unused) in enumerate(ROWS_DOWN):
            put_row(step, DOWN, q, moved[i][source][0:1])
        corner = ((7, 1, 7), (10, 0, 7), (9, 1, 0), (8, 0, 0))
        for q, (i, source, row) in enumerate(corner):
            dsend[step, q] = jnp.broadcast_to(moved[i][source][row : row + 1], (8, 128))
        if step < STEPS - 1:
            for side, sign, row in ((UP, 1, 7), (DOWN, -1, 0)):
                inner = row - sign
                for p in range(2):
                    level = {0: [], sign: []}
                    own = []
                    for i in range(19):
                        source = p - VEL[i][0]
                        if source not in (0, 1):
                            continue
                        if VEL[i][1] in level:
                            level[VEL[i][1]].append((i, moved[i][source]))
                        else:
                            own.append((i, moved[i][source]))
                    for m in range(4):
                        flat = sum_moment(level[0], m)
                        steep = sum_moment(level[sign], m)
                        value = 0.0
                        if flat is not None:
                            value = flat[row : row + 1]
                        if steep is not None:
                            value = value + steep[inner : inner + 1]
                        ysend[side, 1, p * 4 + m : p * 4 + m + 1, :] = value
                        mine = sum_moment(own, m)
                        mown[side, p * 4 + m : p * 4 + m + 1, :] = (
                            jnp.zeros((1, 128), jnp.float32) if mine is None else mine[7 - row : 8 - row]
                        )
                for q, names, source, at in ((0, GO_RIGHT, 1, 0), (1, GO_LEFT, 0, 4)):
                    q = q + (0 if side == UP else 2)
                    flat_set = [(i, moved[i][source]) for i in names if VEL[i][1] == 0]
                    steep_set = [(i, moved[i][source]) for i in names if VEL[i][1] == sign]
                    for m in range(4):
                        flat = sum_moment(flat_set, m)
                        steep = sum_moment(steep_set, m)
                        value = 0.0
                        if flat is not None:
                            value = flat[row : row + 1]
                        if steep is not None:
                            value = value + steep[inner : inner + 1]
                        dsend[step, q, at + m : at + m + 1, :] = value
        for q, where in enumerate(diagonals):
            sent.append(launch(dsend.at[step, q], drecv.at[step, q], d_send.at[step, q], d_recv.at[step, q], where))
        for side, where in ((UP, (s, t_next)), (DOWN, (s, t_prev))):
            if step < STEPS - 1:
                source, target = ysend.at[side], yrecv.at[side]
            else:
                source, target = ylast.at[side], ylast_recv.at[side]
            sent.append(launch(source, target, y_send.at[step, side], y_recv.at[step, side], where))
        return sent

    def sum_moment(members, m):
        if m == 0:
            return add_up((1, value) for i, value in members)
        return add_up((VEL[i][m - 1], value) for i, value in members)

    def stream(step, moved):
        new = []
        for i in range(19):
            cx, cy, unused = VEL[i]
            planes = []
            for p in range(2):
                source = p - cx
                if source in (0, 1):
                    tile = moved[i][source]
                elif cx == 1:
                    tile = xrecv[step, 0, GO_RIGHT.index(i)]
                else:
                    tile = xrecv[step, 1, GO_LEFT.index(i)]
                if cy != 0:
                    side = UP if cy == 1 else DOWN
                    rows = ROWS_UP if cy == 1 else ROWS_DOWN
                    if source in (0, 1):
                        at = rows.index((i, source, p))
                        edge = got_row(step, side, at)
                    else:
                        q = (0 if cx == 1 else 1) + (0 if cy == 1 else 2)
                        at = 4 if cx == 1 else 0
                        edge = drecv[step, q, at : at + 1, :]
                    tile = jnp.where(row_of == (0 if cy == 1 else 7), edge, pltpu.roll(tile, cy % 8, 0))
                planes.append(tile)
            new.append(jnp.stack(planes))
        return new

    def edge_moments(step, side):
        low = row_of < 4
        total = yrecv[side, 1] + mown[side]
        q = 0 if side == UP else 2
        total = total + jnp.where(low, drecv[step, q], drecv[step, q + 1])
        sign = 1 if side == UP else -1
        row = 0 if side == UP else 7
        i = 9 if side == UP else 7
        left = xrecv[step, 0, GO_RIGHT.index(i), row : row + 1, :]
        i = 8 if side == UP else 10
        right = xrecv[step, 1, GO_LEFT.index(i), row : row + 1, :]
        total = total + jnp.where((row_of == 0) | (row_of == 1), left, 0.0)
        total = total + jnp.where(row_of == 2, -sign * left, 0.0)
        total = total + jnp.where(row_of == 4, right, 0.0)
        total = total + jnp.where(row_of == 5, -right, 0.0)
        total = total + jnp.where(row_of == 6, -sign * right, 0.0)
        return total

    def edge_velocity(total):
        values = []
        for p in range(2):
            inv = 1.0 / total[p * 4 : p * 4 + 1]
            values.append(total[p * 4 + 1 : p * 4 + 4] * inv)
        return values

    solid = solid_ref[...]

    g = marker_pass(0)
    moved = deep(collide(f, rho, mom, g, solid))
    for copy in exchange(0, moved):
        copy.wait_recv()
    f = stream(0, moved)
    low = edge_velocity(edge_moments(0, UP))
    high = edge_velocity(edge_moments(0, DOWN))
    for p in range(2):
        hbuf[p, 0:3, :] = low[p]
        hbuf[p, 3:6, :] = high[p]
    rho, mom = moments(f)
    inv = 1.0 / rho
    set_velocity([mom[d] * inv for d in range(3)])

    g = marker_pass(1)

    moved = deep(collide(f, rho, mom, g, solid))
    for copy in exchange(1, moved):
        copy.wait_recv()
    f = stream(1, moved)
    for i in range(19):
        out_ref[i] = f[i]

    def others(action):
        def body(k, carry):
            pl.when(k != t)(functools.partial(action, k))
            return carry

        lax.fori_loop(0, n_trans, body, 0)

    urecv[t] = uret[t]
    others(return_wait)
    vel = [urecv[k] for k in range(n_trans)]
    while len(vel) > 1:
        vel = [vel[k] + vel[k + 1] for k in range(0, len(vel), 2)]
    force_ref[...] = gath[t, 7:8, :] * (gath[t, 4:7, :] - vel[0][0:3])

    for copy in copies:
        copy.wait_send()

    def finish(k):
        gather_copy(k).wait_send()
        return_copy(k).wait_send()

    others(finish)


def per_device(n_stream, n_trans, populations, solid, support, fractions, target, area):
    columns = 4 if n_trans % 32 == 0 else 2
    run = n_trans // columns
    dma = pltpu.SemaphoreType.DMA
    f32 = jnp.float32
    vmem = pl.BlockSpec(memory_space=pltpu.VMEM)
    markers = support.shape[0]
    return pl.pallas_call(
        functools.partial(kernel, n_stream, n_trans, columns),
        out_shape=(
            jax.ShapeDtypeStruct(populations.shape, f32),
            jax.ShapeDtypeStruct((3, markers), f32),
        ),
        in_specs=[pl.BlockSpec(memory_space=pltpu.MemorySpace.HBM)] * 6,
        out_specs=(vmem, vmem),
        scratch_shapes=[
            pltpu.VMEM(populations.shape, f32),
            pltpu.VMEM(solid.shape, jnp.int32),
            pltpu.VMEM((1, markers), jnp.int32),
            pltpu.VMEM((3, markers), f32),
            pltpu.VMEM((3, markers), f32),
            pltpu.VMEM((1, markers), f32),
            pltpu.VMEM((n_trans, 8, 128), f32),
            pltpu.VMEM((columns, 128, run * 128), jnp.bfloat16),
            pltpu.VMEM((128, 256), jnp.bfloat16),
            pltpu.VMEM((2, 8, 128), f32),
            pltpu.VMEM((2, 8, 128), f32),
            pltpu.VMEM((2, 8, 128), f32),
            pltpu.VMEM((2, 2, 5, 8, 128), f32),
            pltpu.VMEM((2, 2, 5, 8, 128), f32),
            pltpu.VMEM((2, 2, 8, 128), f32),
            pltpu.VMEM((2, 2, 8, 128), f32),
            pltpu.VMEM((2, 8, 128), f32),
            pltpu.VMEM((2, 8, 128), f32),
            pltpu.VMEM((2, 8, 128), f32),
            pltpu.VMEM((2, 4, 8, 128), f32),
            pltpu.VMEM((2, 4, 8, 128), f32),
            pltpu.VMEM((n_trans, 3, 128), f32),
            pltpu.VMEM((n_trans, 3, 128), f32),
            dma((6,)),
            dma((n_trans,)),
            dma((n_trans,)),
            dma((2,)),
            dma((2,)),
            dma((2, 2)),
            dma((2, 2)),
            dma((2, 2)),
            dma((2, 2)),
            dma((2, 4)),
            dma((2, 4)),
            dma((n_trans,)),
            dma((n_trans,)),
        ],
        compiler_params=pltpu.CompilerParams(
            collective_id=0, has_side_effects=True, vmem_limit_bytes=56 * 1024 * 1024
        ),
        name="tract",
    )(
        populations,
        solid,
        support.reshape(1, markers),
        fractions,
        target,
        area.reshape(1, markers),
    )


def solution(mesh):
    placed = (
        P(None, "stream", "trans", None),
        P("stream", "trans", None),
        P(("stream", "trans")),
        P(None, ("stream", "trans")),
        P(None, ("stream", "trans")),
        P(("stream", "trans")),
    )
    return jax.shard_map(
        functools.partial(per_device, mesh.shape["stream"], mesh.shape["trans"]),
        mesh=mesh,
        in_specs=placed,
        out_specs=(P(None, "stream", "trans", None), P(None, ("stream", "trans"))),
        check_vma=False,
    )
```

```python
import functools
import math

import jax
import jax.numpy as jnp
from jax import lax
from jax.experimental import pallas as pl
from jax.experimental.pallas import tpu as pltpu
from jax.sharding import PartitionSpec as P

STEPS = 2
VEL = (
    (0, 0, 0),
    (1, 0, 0),
    (-1, 0, 0),
    (0, 1, 0),
    (0, -1, 0),
    (0, 0, 1),
    (0, 0, -1),
    (1, 1, 0),
    (-1, -1, 0),
    (1, -1, 0),
    (-1, 1, 0),
    (1, 0, 1),
    (-1, 0, -1),
    (1, 0, -1),
    (-1, 0, 1),
    (0, 1, 1),
    (0, -1, -1),
    (0, 1, -1),
    (0, -1, 1),
)
WEIGHT = (1.0 / 3.0,) + (1.0 / 18.0,) * 6 + (1.0 / 36.0,) * 12
OPP = (0, 2, 1, 4, 3, 6, 5, 8, 7, 10, 9, 12, 11, 14, 13, 16, 15, 18, 17)
TAU_BASE = 0.8
SMAG = 0.17
MESH = pl.DeviceIdType.MESH
UP = 0
DOWN = 1
GO_RIGHT = (1, 7, 9, 11, 13)
GO_LEFT = (2, 8, 10, 12, 14)
ROWS_UP = ((3, 0, 0), (3, 1, 1), (15, 0, 0), (15, 1, 1), (17, 0, 0), (17, 1, 1), (7, 0, 1), (10, 1, 0))
ROWS_DOWN = ((4, 0, 0), (4, 1, 1), (16, 0, 0), (16, 1, 1), (18, 0, 0), (18, 1, 1), (8, 1, 0), (9, 0, 1))


def add_up(terms):
    total = None
    for sign, value in terms:
        if sign == 0:
            continue
        if total is None:
            total = value if sign > 0 else -value
        else:
            total = total + value if sign > 0 else total - value
    return total


def combine(factors, values):
    total = add_up(zip(factors, values))
    return 0.0 if total is None else total


def moments(f):
    rho = add_up((1, f[i]) for i in range(19))
    mom = [add_up((VEL[i][d], f[i]) for i in range(19)) for d in range(3)]
    return rho, mom


def collide(f, rho, mom, g, solid):
    inv_rho = 1.0 / rho
    u = [(mom[d] + 0.5 * g[d]) * inv_rho for d in range(3)]
    square = u[0] * u[0] + u[1] * u[1] + u[2] * u[2]
    ug = u[0] * g[0] + u[1] * g[1] + u[2] * g[2]
    base = 1.0 - 1.5 * square
    proj = [combine(VEL[i], u) for i in range(19)]
    neq = []
    for i in range(19):
        feq = WEIGHT[i] * rho * (base + 3.0 * proj[i] + 4.5 * proj[i] * proj[i])
        neq.append(f[i] - feq)
    mag2 = 0.0
    for a, b in ((0, 0), (1, 1), (2, 2), (0, 1), (0, 2), (1, 2)):
        comp = combine([VEL[i][a] * VEL[i][b] for i in range(19)], neq)
        mag2 = mag2 + (1.0 if a == b else 2.0) * comp * comp
    mag = jnp.sqrt(mag2)
    tau = 0.5 * (
        TAU_BASE + jnp.sqrt(TAU_BASE * TAU_BASE + 18.0 * math.sqrt(2.0) * SMAG * SMAG * mag * inv_rho)
    )
    inv_tau = 1.0 / tau
    share = 1.0 - 0.5 * inv_tau
    is_solid = solid == 1
    out = []
    for i in range(19):
        cg = combine(VEL[i], g)
        source = share * (WEIGHT[i] * (3.0 * (cg - ug) + 9.0 * proj[i] * cg))
        out.append(jnp.where(is_solid, f[OPP[i]], f[i] - neq[i] * inv_tau + source))
    return out


def split(x, axis):
    hi = x.astype(jnp.bfloat16)
    lo = (x - hi.astype(jnp.float32)).astype(jnp.bfloat16)
    return jnp.concatenate([hi, lo], axis=axis)


def kernel(
    n_stream,
    n_trans,
    columns,
    pop_hbm,
    solid_hbm,
    support_hbm,
    frac_hbm,
    target_hbm,
    area_hbm,
    out_ref,
    force_ref,
    pop_ref,
    solid_ref,
    support_ref,
    frac_ref,
    target_ref,
    area_ref,
    gath,
    onehot,
    vs,
    htile,
    hrecv,
    wrap,
    hbuf,
    xsend,
    xrecv,
    ysend,
    yrecv,
    ylast,
    ylast_recv,
    mown,
    dsend,
    drecv,
    uret,
    urecv,
    in_sem,
    ready,
    w_send,
    w_recv,
    l_send,
    l_recv,
    g_send,
    g_recv,
    h_send,
    h_recv,
    x_send,
    x_recv,
    y_send,
    y_recv,
    d_send,
    d_recv,
    u_send,
    u_recv,
):
    s = lax.axis_index("stream")
    t = lax.axis_index("trans")
    s_next = lax.rem(s + 1, n_stream)
    s_prev = lax.rem(s + n_stream - 1, n_stream)
    t_next = lax.rem(t + 1, n_trans)
    t_prev = lax.rem(t + n_trans - 1, n_trans)
    diagonals = ((s_next, t_next), (s_prev, t_next), (s_next, t_prev), (s_prev, t_prev))

    run = n_trans // columns
    x = t // run
    z = lax.rem(t, run)
    own = z * columns + x
    h = run // 2
    lower = z < h
    half = max(n_stream // 2, 1)
    partners = ((s_next, t), (s_prev, t)) + diagonals + ((s, t_next), (s, t_prev))
    back = (1, 0, 5, 4, 3, 2, 7, 6)

    def height(where):
        return (where[0] // half) * run + lax.rem(where[1], run)

    heights = [height(where) for where in partners]
    level = height((s, t))
    others_x = (2, 1, 3) if columns == 4 else tuple(range(1, columns))

    def column(offset):
        return lax.rem(x + offset, columns)

    loads = [
        pltpu.make_async_copy(source, target, in_sem.at[k])
        for k, (source, target) in enumerate(
            (
                (pop_hbm, pop_ref),
                (support_hbm, support_ref),
                (frac_hbm, frac_ref),
                (target_hbm, target_ref),
                (area_hbm, area_ref),
                (solid_hbm, solid_ref),
            )
        )
    ]
    for load in loads:
        load.start()
    barrier = pltpu.get_barrier_semaphore()

    def greet(where):
        pl.semaphore_signal(barrier, inc=1, device_id=where, device_id_type=MESH)

    expected = jnp.where(lower, h * columns, n_trans) - 1
    for row in range(run):

        @pl.when(lower | (row >= h))
        def _():
            for offset in others_x:
                greet((s, column(offset) * run + row))
            pl.when(row != z)(lambda: greet((s, x * run + row)))

    pl.when(z >= h)(lambda: greet((s, t - h)))
    expected = expected + lower.astype(jnp.int32)
    if h > 1:
        pl.when(z == h)(lambda: greet((s, t_prev)))
        expected = expected + (z == h - 1).astype(jnp.int32)
    pl.when(z == h)(lambda: greet((s, column(1) * run)))
    expected = expected + (z == 0).astype(jnp.int32)
    for where, height_there in zip(partners[:6], heights[:6]):
        pl.when(height_there >= level)(functools.partial(greet, where))
        expected = expected + (height_there <= level).astype(jnp.int32)

    for load in loads[1:5]:
        load.wait()

    gath[own, 0:1, :] = support_ref[...].astype(jnp.float32)
    gath[own, 1:4, :] = frac_ref[...]
    gath[own, 4:7, :] = target_ref[...]
    gath[own, 7:8, :] = area_ref[...]

    loads[0].wait()
    loads[5].wait()
    f = [pop_ref[i] for i in range(19)]
    rho, mom = moments(f)
    inv = 1.0 / rho
    ustar = [mom[d] * inv for d in range(3)]
    htile[...] = jnp.zeros_like(htile)
    for p in range(2):
        for d in range(3):
            htile[UP, p * 4 + d : p * 4 + d + 1, :] = ustar[d][p, 7:8, :]
            htile[DOWN, p * 4 + d : p * 4 + d + 1, :] = ustar[d][p, 0:1, :]

    pl.semaphore_wait(barrier, expected)

    def answer(q):
        pl.semaphore_signal(ready.at[back[q]], inc=1, device_id=partners[q], device_id_type=MESH)

    def await_ready(q):
        pl.semaphore_wait(ready.at[q], 1)

    def remote(src, dst, send, recv, where):
        return pltpu.make_async_remote_copy(
            src_ref=src, dst_ref=dst, send_sem=send, recv_sem=recv, device_id=where, device_id_type=MESH
        )

    copies = []

    def launch(*args):
        copy = remote(*args)
        copy.start()
        copies.append(copy)
        return copy

    def tile_copy(where, slot):
        return remote(gath.at[own], gath.at[own], g_send.at[slot], g_recv.at[own], (s, where))

    def tile_wait(slot):
        remote(gath.at[own], gath.at[slot], g_send.at[slot], g_recv.at[slot], (s, t_next)).wait_recv()

    def level_copy(row, where, k):
        part = gath.at[pl.ds(row * columns, columns)]
        return remote(part, part, l_send.at[k], l_recv.at[row], (s, where))

    def halo_copy(side):
        where = (s, t_next if side == UP else t_prev)
        return remote(htile.at[side], hrecv.at[side], h_send.at[side], h_recv.at[side], where)

    def wrap_copy():
        return remote(
            htile.at[DOWN], wrap, h_send.at[DOWN], w_recv, (s, column(columns - 1) * run + h)
        )

    def wrap_on():
        return remote(wrap, hrecv.at[DOWN], w_send, h_recv.at[DOWN], (s, x * run + run - 1))

    for row in range(run):

        @pl.when((z >= h) | (row < h))
        def _():
            for offset in others_x:
                tile_copy(column(offset) * run + row, row * columns + column(offset)).start()
            pl.when(row != z)(lambda: tile_copy(x * run + row, row * columns + x).start())

    halo_copy(UP).start()
    pl.when(z > 0)(lambda: halo_copy(DOWN).start())
    pl.when(z == 0)(lambda: wrap_copy().start())

    @pl.when(lower)
    def _():
        for offset in others_x:
            tile_wait(z * columns + column(offset))
        level_copy(z, t + h, z).start()

    for row in range(h):

        @pl.when(row == z - h)
        def _():
            level_copy(row, t_next, row).wait_recv()
            for k in range(h):
                if k != row:
                    level_copy(row, x * run + h + k, k).start()

    @pl.when(z == h)
    def _():
        wrap_copy().wait_recv()
        wrap_on().start()

    for q in range(6):
        pl.when(heights[q] < level)(functools.partial(answer, q))
    halo_copy(UP).wait_recv()
    halo_copy(DOWN).wait_recv()

    hbuf[...] = jnp.zeros_like(hbuf)

    def set_halo(lo, hi):
        for p in range(2):
            hbuf[p, 0:3, :] = lo[p * 4 : p * 4 + 3, :]
            hbuf[p, 3:6, :] = hi[p * 4 : p * 4 + 3, :]

    def set_velocity(ustar):
        rows = []
        for shift in (0, 1):
            for d in range(3):
                for p in range(2):
                    x = ustar[d][p]
                    rows.append(pltpu.roll(x, 127, 1) if shift else x)
        for shift in (0, 1):
            for p in range(2):
                x = hbuf[p]
                rows.append(pltpu.roll(x, 127, 1) if shift else x)
        vs[...] = split(jnp.concatenate(rows, axis=0), 1)

    set_halo(hrecv[UP], hrecv[DOWN])
    set_velocity(ustar)

    tiles = n_trans // columns
    width = tiles * 128
    rows_of = tiles // columns
    first_row = (t * 8).astype(jnp.float32)

    def return_copy(where, slot):
        return remote(uret.at[slot], urecv.at[own], u_send.at[slot], u_recv.at[own], (s, where))

    def return_wait(slot):
        remote(uret.at[slot], urecv.at[slot], u_send.at[slot], u_recv.at[slot], (s, t_next)).wait_recv()

    def marker_pass(step):
        def chunk(j):
            first = j * tiles
            rows = range(j * rows_of, (j + 1) * rows_of)
            if step == 0:
                for row in rows:
                    if row < h:

                        @pl.when(lower & (row != z))
                        def _():
                            for offset in range(columns):
                                tile_wait(row * columns + offset)

                        pl.when((z >= h) & (row != z - h))(
                            lambda: level_copy(row, t_next, 0).wait_recv()
                        )
                    else:
                        for offset in others_x:
                            tile_wait(row * columns + column(offset))
                        pl.when(row != z)(lambda: tile_wait(row * columns + x))

            tile = jnp.concatenate([gath[first + i] for i in range(tiles)], axis=1)
            fx, fy, fz = tile[1:2], tile[2:3], tile[3:4]
            b = jnp.floor(tile[0:1] * (1.0 / 128.0))
            if step == 0:
                e = tile[0:1] - 128.0 * b
                depth = lax.broadcasted_iota(jnp.int32, (128, width), 0).astype(jnp.float32)
                pick = jnp.where(depth == e, 1.0, 0.0).astype(jnp.bfloat16)
                onehot[j] = pick
            else:
                pick = onehot[j]
            r = lax.dot_general(
                vs[...],
                jnp.concatenate([pick, pick], axis=0),
                (((1,), (0,)), ((), ())),
                preferred_element_type=jnp.float32,
            )
            gx, gy, gz = 1.0 - fx, 1.0 - fy, 1.0 - fz
            local = lax.broadcasted_iota(jnp.int32, (8, width), 0).astype(jnp.float32)
            rel = b - first_row
            wy = jnp.where(local == rel, gy, 0.0) + jnp.where(local == rel + 1.0, fy, 0.0)
            wh = jnp.where(
                local < 3.0, jnp.where(rel == -1.0, gy, 0.0), jnp.where(rel == 7.0, fy, 0.0)
            )

            def lerp(at):
                planes = []
                for p in range(2):
                    low, high = at(0, p), at(1, p)
                    planes.append(low * gz + high * fz)
                return planes[0] * gx + planes[1] * fx

            edge = wh * lerp(lambda shift, p: r[(12 + shift * 2 + p) * 8 : (12 + shift * 2 + p) * 8 + 8])
            vel = []
            for d in range(3):
                own = lerp(
                    lambda shift, p: r[((shift * 3 + d) * 2 + p) * 8 : ((shift * 3 + d) * 2 + p) * 8 + 8]
                )
                vel.append(
                    jnp.sum(wy * own, axis=0, keepdims=True) + edge[d : d + 1] + edge[3 + d : 4 + d]
                )
            if step == STEPS - 1:
                mine = (rel >= 0.0) & (rel <= 7.0)
                for d in range(3):
                    back_to = jnp.where(mine, vel[d], 0.0)
                    for i in range(tiles):
                        uret[first + i, d : d + 1, :] = back_to[:, i * 128 : i * 128 + 128]
                for row in rows:
                    for offset in others_x:
                        return_copy(column(offset) * run + row, row * columns + column(offset)).start()
                    pl.when(row != z)(lambda: return_copy(x * run + row, row * columns + x).start())
            spread = []
            wyz = [wy * gz, wy * fz]
            wx = (gx, fx)
            pushes = [tile[7:8] * (tile[4 + d : 5 + d] - vel[d]) for d in range(3)]
            for shift in (0, 1):
                for d in range(3):
                    for p in range(2):
                        spread.append(wyz[shift] * (pushes[d] * wx[p]))
            return lax.dot_general(
                split(jnp.concatenate(spread, axis=0), 0),
                pick,
                (((1,), (1,)), ((), ())),
                preferred_element_type=jnp.float32,
            )

        total = None
        for j in range(columns):
            part = chunk(j)
            total = part if total is None else total + part
        total = total[0:96] + total[96:192]
        g = []
        for d in range(3):
            planes = []
            for p in range(2):
                low = total[(d * 2 + p) * 8 : (d * 2 + p) * 8 + 8]
                high = total[((3 + d) * 2 + p) * 8 : ((3 + d) * 2 + p) * 8 + 8]
                planes.append(low + pltpu.roll(high, 1, 1))
            g.append(jnp.stack(planes))
        return g

    row_of = lax.broadcasted_iota(jnp.int32, (8, 128), 0)

    def deep(post):
        return [
            [
                pltpu.roll(post[i][p], VEL[i][2] % 128, 1) if VEL[i][2] else post[i][p]
                for p in range(2)
            ]
            for i in range(19)
        ]

    def put_row(step, side, at, value):
        if step < STEPS - 1:
            ysend[side, 0, at : at + 1, :] = value
        else:
            ylast[side, at : at + 1, :] = value

    def got_row(step, side, at):
        if step < STEPS - 1:
            return yrecv[side, 0, at : at + 1, :]
        return ylast_recv[side, at : at + 1, :]

    def exchange(step, moved):
        sent = []
        for q, i in enumerate(GO_RIGHT):
            xsend[step, 0, q] = moved[i][1]
        for q, i in enumerate(GO_LEFT):
            xsend[step, 1, q] = moved[i][0]
        sent.append(launch(xsend.at[step, 0], xrecv.at[step, 0], x_send.at[step, 0], x_recv.at[step, 0], (s_next, t)))
        sent.append(launch(xsend.at[step, 1], xrecv.at[step, 1], x_send.at[step, 1], x_recv.at[step, 1], (s_prev, t)))
        for q, (i, source, unused) in enumerate(ROWS_UP):
            put_row(step, UP, q, moved[i][source][7:8])
        for q, (i, source, unused) in enumerate(ROWS_DOWN):
            put_row(step, DOWN, q, moved[i][source][0:1])
        corner = ((7, 1, 7), (10, 0, 7), (9, 1, 0), (8, 0, 0))
        for q, (i, source, row) in enumerate(corner):
            dsend[step, q] = jnp.broadcast_to(moved[i][source][row : row + 1], (8, 128))
        if step < STEPS - 1:
            for side, sign, row in ((UP, 1, 7), (DOWN, -1, 0)):
                inner = row - sign
                for p in range(2):
                    level = {0: [], sign: []}
                    own = []
                    for i in range(19):
                        source = p - VEL[i][0]
                        if source not in (0, 1):
                            continue
                        if VEL[i][1] in level:
                            level[VEL[i][1]].append((i, moved[i][source]))
                        else:
                            own.append((i, moved[i][source]))
                    for m in range(4):
                        flat = sum_moment(level[0], m)
                        steep = sum_moment(level[sign], m)
                        value = 0.0
                        if flat is not None:
                            value = flat[row : row + 1]
                        if steep is not None:
                            value = value + steep[inner : inner + 1]
                        ysend[side, 1, p * 4 + m : p * 4 + m + 1, :] = value
                        mine = sum_moment(own, m)
                        mown[side, p * 4 + m : p * 4 + m + 1, :] = (
                            jnp.zeros((1, 128), jnp.float32) if mine is None else mine[7 - row : 8 - row]
                        )
                for q, names, source, at in ((0, GO_RIGHT, 1, 0), (1, GO_LEFT, 0, 4)):
                    q = q + (0 if side == UP else 2)
                    flat_set = [(i, moved[i][source]) for i in names if VEL[i][1] == 0]
                    steep_set = [(i, moved[i][source]) for i in names if VEL[i][1] == sign]
                    for m in range(4):
                        flat = sum_moment(flat_set, m)
                        steep = sum_moment(steep_set, m)
                        value = 0.0
                        if flat is not None:
                            value = flat[row : row + 1]
                        if steep is not None:
                            value = value + steep[inner : inner + 1]
                        dsend[step, q, at + m : at + m + 1, :] = value
        for q, where in enumerate(diagonals):
            sent.append(launch(dsend.at[step, q], drecv.at[step, q], d_send.at[step, q], d_recv.at[step, q], where))
        for side, where in ((UP, (s, t_next)), (DOWN, (s, t_prev))):
            if step < STEPS - 1:
                source, target = ysend.at[side], yrecv.at[side]
            else:
                source, target = ylast.at[side], ylast_recv.at[side]
            sent.append(launch(source, target, y_send.at[step, side], y_recv.at[step, side], where))
        return sent

    def sum_moment(members, m):
        if m == 0:
            return add_up((1, value) for i, value in members)
        return add_up((VEL[i][m - 1], value) for i, value in members)

    def stream(step, moved):
        new = []
        for i in range(19):
            cx, cy, unused = VEL[i]
            planes = []
            for p in range(2):
                source = p - cx
                if source in (0, 1):
                    tile = moved[i][source]
                elif cx == 1:
                    tile = xrecv[step, 0, GO_RIGHT.index(i)]
                else:
                    tile = xrecv[step, 1, GO_LEFT.index(i)]
                if cy != 0:
                    side = UP if cy == 1 else DOWN
                    rows = ROWS_UP if cy == 1 else ROWS_DOWN
                    if source in (0, 1):
                        at = rows.index((i, source, p))
                        edge = got_row(step, side, at)
                    else:
                        q = (0 if cx == 1 else 1) + (0 if cy == 1 else 2)
                        at = 4 if cx == 1 else 0
                        edge = drecv[step, q, at : at + 1, :]
                    tile = jnp.where(row_of == (0 if cy == 1 else 7), edge, pltpu.roll(tile, cy % 8, 0))
                planes.append(tile)
            new.append(jnp.stack(planes))
        return new

    def edge_moments(step, side):
        low = row_of < 4
        total = yrecv[side, 1] + mown[side]
        q = 0 if side == UP else 2
        total = total + jnp.where(low, drecv[step, q], drecv[step, q + 1])
        sign = 1 if side == UP else -1
        row = 0 if side == UP else 7
        i = 9 if side == UP else 7
        left = xrecv[step, 0, GO_RIGHT.index(i), row : row + 1, :]
        i = 8 if side == UP else 10
        right = xrecv[step, 1, GO_LEFT.index(i), row : row + 1, :]
        total = total + jnp.where((row_of == 0) | (row_of == 1), left, 0.0)
        total = total + jnp.where(row_of == 2, -sign * left, 0.0)
        total = total + jnp.where(row_of == 4, right, 0.0)
        total = total + jnp.where(row_of == 5, -right, 0.0)
        total = total + jnp.where(row_of == 6, -sign * right, 0.0)
        return total

    def edge_velocity(total):
        values = []
        for p in range(2):
            inv = 1.0 / total[p * 4 : p * 4 + 1]
            values.append(total[p * 4 + 1 : p * 4 + 4] * inv)
        return values

    solid = solid_ref[...]

    g = marker_pass(0)
    moved = deep(collide(f, rho, mom, g, solid))
    for q in range(6):
        pl.when(heights[q] > level)(functools.partial(await_ready, q))
    for copy in exchange(0, moved):
        copy.wait_recv()
    f = stream(0, moved)
    low = edge_velocity(edge_moments(0, UP))
    high = edge_velocity(edge_moments(0, DOWN))
    for p in range(2):
        hbuf[p, 0:3, :] = low[p]
        hbuf[p, 3:6, :] = high[p]
    rho, mom = moments(f)
    inv = 1.0 / rho
    set_velocity([mom[d] * inv for d in range(3)])

    g = marker_pass(1)

    moved = deep(collide(f, rho, mom, g, solid))
    for copy in exchange(1, moved):
        copy.wait_recv()
    f = stream(1, moved)
    for i in range(19):
        out_ref[i] = f[i]

    urecv[own] = uret[own]

    def others(action):
        for row in range(run):
            for offset in others_x:
                action(row * columns + column(offset))
            pl.when(row != z)(functools.partial(action, row * columns + x))

    others(return_wait)
    vel = [urecv[k] for k in range(n_trans)]
    while len(vel) > 1:
        vel = [vel[k] + vel[k + 1] for k in range(0, len(vel), 2)]
    force_ref[...] = gath[own, 7:8, :] * (gath[own, 4:7, :] - vel[0][0:3])

    for copy in copies:
        copy.wait_send()

    halo_copy(UP).wait_send()
    halo_copy(DOWN).wait_send()
    pl.when(z == h)(lambda: wrap_on().wait_send())
    for row in range(run):

        @pl.when((z >= h) | (row < h))
        def _():
            for offset in others_x:
                tile_copy(t_next, row * columns + column(offset)).wait_send()
            pl.when(row != z)(lambda: tile_copy(t_next, row * columns + x).wait_send())

    pl.when(lower)(lambda: level_copy(z, t_next, z).wait_send())
    for k in range(h):
        pl.when((z >= h) & (k != z - h))(lambda: level_copy(0, t_next, k).wait_send())
    others(lambda slot: return_copy(t_next, slot).wait_send())


def per_device(n_stream, n_trans, populations, solid, support, fractions, target, area):
    columns = 4 if n_trans % 32 == 0 else 2
    run = n_trans // columns
    dma = pltpu.SemaphoreType.DMA
    f32 = jnp.float32
    vmem = pl.BlockSpec(memory_space=pltpu.VMEM)
    markers = support.shape[0]
    return pl.pallas_call(
        functools.partial(kernel, n_stream, n_trans, columns),
        out_shape=(
            jax.ShapeDtypeStruct(populations.shape, f32),
            jax.ShapeDtypeStruct((3, markers), f32),
        ),
        in_specs=[pl.BlockSpec(memory_space=pltpu.MemorySpace.HBM)] * 6,
        out_specs=(vmem, vmem),
        scratch_shapes=[
            pltpu.VMEM(populations.shape, f32),
            pltpu.VMEM(solid.shape, jnp.int32),
            pltpu.VMEM((1, markers), jnp.int32),
            pltpu.VMEM((3, markers), f32),
            pltpu.VMEM((3, markers), f32),
            pltpu.VMEM((1, markers), f32),
            pltpu.VMEM((n_trans, 8, 128), f32),
            pltpu.VMEM((columns, 128, run * 128), jnp.bfloat16),
            pltpu.VMEM((128, 256), jnp.bfloat16),
            pltpu.VMEM((2, 8, 128), f32),
            pltpu.VMEM((2, 8, 128), f32),
            pltpu.VMEM((8, 128), f32),
            pltpu.VMEM((2, 8, 128), f32),
            pltpu.VMEM((2, 2, 5, 8, 128), f32),
            pltpu.VMEM((2, 2, 5, 8, 128), f32),
            pltpu.VMEM((2, 2, 8, 128), f32),
            pltpu.VMEM((2, 2, 8, 128), f32),
            pltpu.VMEM((2, 8, 128), f32),
            pltpu.VMEM((2, 8, 128), f32),
            pltpu.VMEM((2, 8, 128), f32),
            pltpu.VMEM((2, 4, 8, 128), f32),
            pltpu.VMEM((2, 4, 8, 128), f32),
            pltpu.VMEM((n_trans, 3, 128), f32),
            pltpu.VMEM((n_trans, 3, 128), f32),
            dma((6,)),
            pltpu.SemaphoreType.REGULAR((8,)),
            dma,
            dma,
            dma((run,)),
            dma((run,)),
            dma((n_trans,)),
            dma((n_trans,)),
            dma((2,)),
            dma((2,)),
            dma((2, 2)),
            dma((2, 2)),
            dma((2, 2)),
            dma((2, 2)),
            dma((2, 4)),
            dma((2, 4)),
            dma((n_trans,)),
            dma((n_trans,)),
        ],
        compiler_params=pltpu.CompilerParams(
            collective_id=0, has_side_effects=True, vmem_limit_bytes=56 * 1024 * 1024
        ),
        name="tract",
    )(
        populations,
        solid,
        support.reshape(1, markers),
        fractions,
        target,
        area.reshape(1, markers),
    )


def solution(mesh):
    placed = (
        P(None, "stream", "trans", None),
        P("stream", "trans", None),
        P(("stream", "trans")),
        P(None, ("stream", "trans")),
        P(None, ("stream", "trans")),
        P(("stream", "trans")),
    )
    return jax.shard_map(
        functools.partial(per_device, mesh.shape["stream"], mesh.shape["trans"]),
        mesh=mesh,
        in_specs=placed,
        out_specs=(P(None, "stream", "trans", None), P(None, ("stream", "trans"))),
        check_vma=False,
    )
```

```python
import functools
import math

import jax
import jax.numpy as jnp
from jax import lax
from jax.experimental import pallas as pl
from jax.experimental.pallas import tpu as pltpu
from jax.sharding import PartitionSpec as P

STEPS = 2
VEL = (
    (0, 0, 0),
    (1, 0, 0),
    (-1, 0, 0),
    (0, 1, 0),
    (0, -1, 0),
    (0, 0, 1),
    (0, 0, -1),
    (1, 1, 0),
    (-1, -1, 0),
    (1, -1, 0),
    (-1, 1, 0),
    (1, 0, 1),
    (-1, 0, -1),
    (1, 0, -1),
    (-1, 0, 1),
    (0, 1, 1),
    (0, -1, -1),
    (0, 1, -1),
    (0, -1, 1),
)
WEIGHT = (1.0 / 3.0,) + (1.0 / 18.0,) * 6 + (1.0 / 36.0,) * 12
OPP = (0, 2, 1, 4, 3, 6, 5, 8, 7, 10, 9, 12, 11, 14, 13, 16, 15, 18, 17)
TAU_BASE = 0.8
SMAG = 0.17
MESH = pl.DeviceIdType.MESH
UP = 0
DOWN = 1
GO_RIGHT = (1, 7, 9, 11, 13)
GO_LEFT = (2, 8, 10, 12, 14)
ROWS_UP = ((3, 0, 0), (3, 1, 1), (15, 0, 0), (15, 1, 1), (17, 0, 0), (17, 1, 1), (7, 0, 1), (10, 1, 0))
ROWS_DOWN = ((4, 0, 0), (4, 1, 1), (16, 0, 0), (16, 1, 1), (18, 0, 0), (18, 1, 1), (8, 1, 0), (9, 0, 1))


def add_up(terms):
    total = None
    for sign, value in terms:
        if sign == 0:
            continue
        if total is None:
            total = value if sign > 0 else -value
        else:
            total = total + value if sign > 0 else total - value
    return total


def combine(factors, values):
    total = add_up(zip(factors, values))
    return 0.0 if total is None else total


def moments(f):
    rho = add_up((1, f[i]) for i in range(19))
    mom = [add_up((VEL[i][d], f[i]) for i in range(19)) for d in range(3)]
    return rho, mom


def collide(f, rho, mom, g, solid):
    inv_rho = 1.0 / rho
    u = [(mom[d] + 0.5 * g[d]) * inv_rho for d in range(3)]
    square = u[0] * u[0] + u[1] * u[1] + u[2] * u[2]
    ug = u[0] * g[0] + u[1] * g[1] + u[2] * g[2]
    base = 1.0 - 1.5 * square
    proj = [combine(VEL[i], u) for i in range(19)]
    neq = []
    for i in range(19):
        feq = WEIGHT[i] * rho * (base + 3.0 * proj[i] + 4.5 * proj[i] * proj[i])
        neq.append(f[i] - feq)
    mag2 = 0.0
    for a, b in ((0, 0), (1, 1), (2, 2), (0, 1), (0, 2), (1, 2)):
        comp = combine([VEL[i][a] * VEL[i][b] for i in range(19)], neq)
        mag2 = mag2 + (1.0 if a == b else 2.0) * comp * comp
    mag = jnp.sqrt(mag2)
    tau = 0.5 * (
        TAU_BASE + jnp.sqrt(TAU_BASE * TAU_BASE + 18.0 * math.sqrt(2.0) * SMAG * SMAG * mag * inv_rho)
    )
    inv_tau = 1.0 / tau
    share = 1.0 - 0.5 * inv_tau
    is_solid = solid == 1
    out = []
    for i in range(19):
        cg = combine(VEL[i], g)
        source = share * (WEIGHT[i] * (3.0 * (cg - ug) + 9.0 * proj[i] * cg))
        out.append(jnp.where(is_solid, f[OPP[i]], f[i] - neq[i] * inv_tau + source))
    return out


def split(x, axis):
    hi = x.astype(jnp.bfloat16)
    lo = (x - hi.astype(jnp.float32)).astype(jnp.bfloat16)
    return jnp.concatenate([hi, lo], axis=axis)


def kernel(
    n_stream,
    n_trans,
    columns,
    pop_hbm,
    solid_hbm,
    support_hbm,
    frac_hbm,
    target_hbm,
    area_hbm,
    out_ref,
    force_ref,
    pop_ref,
    solid_ref,
    support_ref,
    frac_ref,
    target_ref,
    area_ref,
    gath,
    onehot,
    vs,
    htile,
    hrecv,
    wrap,
    hbuf,
    xsend,
    xrecv,
    ysend,
    yrecv,
    ylast,
    ylast_recv,
    mown,
    dsend,
    drecv,
    uret,
    urecv,
    in_sem,
    ready,
    w_send,
    w_recv,
    l_send,
    l_recv,
    g_send,
    g_recv,
    h_send,
    h_recv,
    x_send,
    x_recv,
    y_send,
    y_recv,
    d_send,
    d_recv,
    u_send,
    u_recv,
):
    s = lax.axis_index("stream")
    t = lax.axis_index("trans")
    s_next = lax.rem(s + 1, n_stream)
    s_prev = lax.rem(s + n_stream - 1, n_stream)
    t_next = lax.rem(t + 1, n_trans)
    t_prev = lax.rem(t + n_trans - 1, n_trans)
    diagonals = ((s_next, t_next), (s_prev, t_next), (s_next, t_prev), (s_prev, t_prev))

    run = n_trans // columns
    x = t // run
    z = lax.rem(t, run)
    own = z * columns + x
    h = run // 2
    lower = z < h
    half = max(n_stream // 2, 1)
    partners = ((s_next, t), (s_prev, t)) + diagonals + ((s, t_next), (s, t_prev))
    back = (1, 0, 5, 4, 3, 2, 7, 6)

    def height(where):
        return (where[0] // half) * run + lax.rem(where[1], run)

    heights = [height(where) for where in partners]
    level = height((s, t))
    others_x = (2, 1, 3) if columns == 4 else tuple(range(1, columns))

    def column(offset):
        return lax.rem(x + offset, columns)

    loads = [
        pltpu.make_async_copy(source, target, in_sem.at[k])
        for k, (source, target) in enumerate(
            (
                (pop_hbm, pop_ref),
                (support_hbm, support_ref),
                (frac_hbm, frac_ref),
                (target_hbm, target_ref),
                (area_hbm, area_ref),
                (solid_hbm, solid_ref),
            )
        )
    ]
    for load in loads:
        load.start()
    barrier = pltpu.get_barrier_semaphore()

    def greet(where):
        pl.semaphore_signal(barrier, inc=1, device_id=where, device_id_type=MESH)

    expected = jnp.where(lower, h * columns, n_trans) - 1
    for row in range(run):

        @pl.when(lower | (row >= h))
        def _():
            for offset in others_x:
                greet((s, column(offset) * run + row))
            pl.when(row != z)(lambda: greet((s, x * run + row)))

    pl.when(z >= h)(lambda: greet((s, t - h)))
    expected = expected + lower.astype(jnp.int32)
    if h > 1:
        pl.when(z == h)(lambda: greet((s, t_prev)))
        expected = expected + (z == h - 1).astype(jnp.int32)
    pl.when(z == h)(lambda: greet((s, column(1) * run)))
    expected = expected + (z == 0).astype(jnp.int32)
    for where, height_there in zip(partners[:6], heights[:6]):
        pl.when(height_there >= level)(functools.partial(greet, where))
        expected = expected + (height_there <= level).astype(jnp.int32)

    for load in loads[1:5]:
        load.wait()

    gath[own, 0:1, :] = support_ref[...].astype(jnp.float32)
    gath[own, 1:4, :] = frac_ref[...]
    gath[own, 4:7, :] = target_ref[...]
    gath[own, 7:8, :] = area_ref[...]

    loads[0].wait()
    loads[5].wait()
    f = [pop_ref[i] for i in range(19)]
    rho, mom = moments(f)
    inv = 1.0 / rho
    ustar = [mom[d] * inv for d in range(3)]
    htile[...] = jnp.zeros_like(htile)
    for p in range(2):
        for d in range(3):
            htile[UP, p * 4 + d : p * 4 + d + 1, :] = ustar[d][p, 7:8, :]
            htile[DOWN, p * 4 + d : p * 4 + d + 1, :] = ustar[d][p, 0:1, :]

    pl.semaphore_wait(barrier, expected)

    def answer(q):
        pl.semaphore_signal(ready.at[back[q]], inc=1, device_id=partners[q], device_id_type=MESH)

    def await_ready(q):
        pl.semaphore_wait(ready.at[q], 1)

    def remote(src, dst, send, recv, where):
        return pltpu.make_async_remote_copy(
            src_ref=src, dst_ref=dst, send_sem=send, recv_sem=recv, device_id=where, device_id_type=MESH
        )

    def launch(*args):
        copy = remote(*args)
        copy.start()
        return copy

    def tile_copy(where, slot):
        return remote(gath.at[own], gath.at[own], g_send.at[slot], g_recv.at[own], (s, where))

    def tile_wait(slot):
        remote(gath.at[own], gath.at[slot], g_send.at[slot], g_recv.at[slot], (s, t_next)).wait_recv()

    def level_copy(row, where, k):
        part = gath.at[pl.ds(row * columns, columns)]
        return remote(part, part, l_send.at[k], l_recv.at[row], (s, where))

    def halo_copy(side):
        where = (s, t_next if side == UP else t_prev)
        return remote(htile.at[side], hrecv.at[side], h_send.at[side], h_recv.at[side], where)

    def wrap_copy():
        return remote(
            htile.at[DOWN], wrap, h_send.at[DOWN], w_recv, (s, column(columns - 1) * run + h)
        )

    def wrap_on():
        return remote(wrap, hrecv.at[DOWN], w_send, h_recv.at[DOWN], (s, x * run + run - 1))

    for row in range(run):

        @pl.when((z >= h) | (row < h))
        def _():
            for offset in others_x:
                tile_copy(column(offset) * run + row, row * columns + column(offset)).start()
            pl.when(row != z)(lambda: tile_copy(x * run + row, row * columns + x).start())

    halo_copy(UP).start()
    pl.when(z > 0)(lambda: halo_copy(DOWN).start())
    pl.when(z == 0)(lambda: wrap_copy().start())

    @pl.when(lower)
    def _():
        for offset in others_x:
            tile_wait(z * columns + column(offset))
        level_copy(z, t + h, z).start()

    for row in range(h):

        @pl.when(row == z - h)
        def _():
            level_copy(row, t_next, row).wait_recv()
            for k in range(h):
                if k != row:
                    level_copy(row, x * run + h + k, k).start()

    @pl.when(z == h)
    def _():
        wrap_copy().wait_recv()
        wrap_on().start()

    for q in range(6):
        pl.when(heights[q] < level)(functools.partial(answer, q))
    halo_copy(UP).wait_recv()
    halo_copy(DOWN).wait_recv()

    hbuf[...] = jnp.zeros_like(hbuf)

    def set_halo(lo, hi):
        for p in range(2):
            hbuf[p, 0:3, :] = lo[p * 4 : p * 4 + 3, :]
            hbuf[p, 3:6, :] = hi[p * 4 : p * 4 + 3, :]

    def set_velocity(ustar):
        rows = []
        for shift in (0, 1):
            for d in range(3):
                for p in range(2):
                    x = ustar[d][p]
                    rows.append(pltpu.roll(x, 127, 1) if shift else x)
        for shift in (0, 1):
            for p in range(2):
                x = hbuf[p]
                rows.append(pltpu.roll(x, 127, 1) if shift else x)
        vs[...] = split(jnp.concatenate(rows, axis=0), 1)

    set_halo(hrecv[UP], hrecv[DOWN])
    set_velocity(ustar)

    tiles = n_trans // columns
    width = tiles * 128
    rows_of = tiles // columns
    first_row = (t * 8).astype(jnp.float32)

    def return_copy(where, slot):
        return remote(uret.at[slot], urecv.at[own], u_send.at[slot], u_recv.at[own], (s, where))

    def return_wait(slot):
        remote(uret.at[slot], urecv.at[slot], u_send.at[slot], u_recv.at[slot], (s, t_next)).wait_recv()

    def marker_pass(step):
        def chunk(j):
            first = j * tiles
            rows = range(j * rows_of, (j + 1) * rows_of)
            if step == 0:
                for row in rows:
                    if row < h:

                        @pl.when(lower & (row != z))
                        def _():
                            for offset in range(columns):
                                tile_wait(row * columns + offset)

                        pl.when((z >= h) & (row != z - h))(
                            lambda: level_copy(row, t_next, 0).wait_recv()
                        )
                    else:
                        for offset in others_x:
                            tile_wait(row * columns + column(offset))
                        pl.when(row != z)(lambda: tile_wait(row * columns + x))

            tile = jnp.concatenate([gath[first + i] for i in range(tiles)], axis=1)
            fx, fy, fz = tile[1:2], tile[2:3], tile[3:4]
            b = jnp.floor(tile[0:1] * (1.0 / 128.0))
            if step == 0:
                e = tile[0:1] - 128.0 * b
                depth = lax.broadcasted_iota(jnp.int32, (128, width), 0).astype(jnp.float32)
                pick = jnp.where(depth == e, 1.0, 0.0).astype(jnp.bfloat16)
                onehot[j] = pick
            else:
                pick = onehot[j]
            r = lax.dot_general(
                vs[...],
                jnp.concatenate([pick, pick], axis=0),
                (((1,), (0,)), ((), ())),
                preferred_element_type=jnp.float32,
            )
            gx, gy, gz = 1.0 - fx, 1.0 - fy, 1.0 - fz
            local = lax.broadcasted_iota(jnp.int32, (8, width), 0).astype(jnp.float32)
            rel = b - first_row
            wy = jnp.where(local == rel, gy, 0.0) + jnp.where(local == rel + 1.0, fy, 0.0)
            wh = jnp.where(
                local < 3.0, jnp.where(rel == -1.0, gy, 0.0), jnp.where(rel == 7.0, fy, 0.0)
            )

            def lerp(at):
                planes = []
                for p in range(2):
                    low, high = at(0, p), at(1, p)
                    planes.append(low * gz + high * fz)
                return planes[0] * gx + planes[1] * fx

            edge = wh * lerp(lambda shift, p: r[(12 + shift * 2 + p) * 8 : (12 + shift * 2 + p) * 8 + 8])
            vel = []
            for d in range(3):
                own = lerp(
                    lambda shift, p: r[((shift * 3 + d) * 2 + p) * 8 : ((shift * 3 + d) * 2 + p) * 8 + 8]
                )
                vel.append(
                    jnp.sum(wy * own, axis=0, keepdims=True) + edge[d : d + 1] + edge[3 + d : 4 + d]
                )
            if step == STEPS - 1:
                mine = (rel >= 0.0) & (rel <= 7.0)
                for d in range(3):
                    back_to = jnp.where(mine, vel[d], 0.0)
                    for i in range(tiles):
                        uret[first + i, d : d + 1, :] = back_to[:, i * 128 : i * 128 + 128]
            spread = []
            wyz = [wy * gz, wy * fz]
            wx = (gx, fx)
            pushes = [tile[7:8] * (tile[4 + d : 5 + d] - vel[d]) for d in range(3)]
            for shift in (0, 1):
                for d in range(3):
                    for p in range(2):
                        spread.append(wyz[shift] * (pushes[d] * wx[p]))
            return lax.dot_general(
                split(jnp.concatenate(spread, axis=0), 0),
                pick,
                (((1,), (1,)), ((), ())),
                preferred_element_type=jnp.float32,
            )

        total = None
        for j in range(columns):
            part = chunk(j)
            total = part if total is None else total + part
        total = total[0:96] + total[96:192]
        g = []
        for d in range(3):
            planes = []
            for p in range(2):
                low = total[(d * 2 + p) * 8 : (d * 2 + p) * 8 + 8]
                high = total[((3 + d) * 2 + p) * 8 : ((3 + d) * 2 + p) * 8 + 8]
                planes.append(low + pltpu.roll(high, 1, 1))
            g.append(jnp.stack(planes))
        return g

    row_of = lax.broadcasted_iota(jnp.int32, (8, 128), 0)

    def deep(post):
        return [
            [
                pltpu.roll(post[i][p], VEL[i][2] % 128, 1) if VEL[i][2] else post[i][p]
                for p in range(2)
            ]
            for i in range(19)
        ]

    def put_row(step, side, at, value):
        if step < STEPS - 1:
            ysend[side, 0, at : at + 1, :] = value
        else:
            ylast[side, at : at + 1, :] = value

    def got_row(step, side, at):
        if step < STEPS - 1:
            return yrecv[side, 0, at : at + 1, :]
        return ylast_recv[side, at : at + 1, :]

    def exchange(step, moved):
        sent = []
        for q, i in enumerate(GO_RIGHT):
            xsend[step, 0, q] = moved[i][1]
        for q, i in enumerate(GO_LEFT):
            xsend[step, 1, q] = moved[i][0]
        sent.append(launch(xsend.at[step, 0], xrecv.at[step, 0], x_send.at[step, 0], x_recv.at[step, 0], (s_next, t)))
        sent.append(launch(xsend.at[step, 1], xrecv.at[step, 1], x_send.at[step, 1], x_recv.at[step, 1], (s_prev, t)))
        for q, (i, source, unused) in enumerate(ROWS_UP):
            put_row(step, UP, q, moved[i][source][7:8])
        for q, (i, source, unused) in enumerate(ROWS_DOWN):
            put_row(step, DOWN, q, moved[i][source][0:1])
        corner = ((7, 1, 7), (10, 0, 7), (9, 1, 0), (8, 0, 0))
        for q, (i, source, row) in enumerate(corner):
            dsend[step, q] = jnp.broadcast_to(moved[i][source][row : row + 1], (8, 128))
        if step < STEPS - 1:
            for side, sign, row in ((UP, 1, 7), (DOWN, -1, 0)):
                inner = row - sign
                for p in range(2):
                    level = {0: [], sign: []}
                    own = []
                    for i in range(19):
                        source = p - VEL[i][0]
                        if source not in (0, 1):
                            continue
                        if VEL[i][1] in level:
                            level[VEL[i][1]].append((i, moved[i][source]))
                        else:
                            own.append((i, moved[i][source]))
                    for m in range(4):
                        flat = sum_moment(level[0], m)
                        steep = sum_moment(level[sign], m)
                        value = 0.0
                        if flat is not None:
                            value = flat[row : row + 1]
                        if steep is not None:
                            value = value + steep[inner : inner + 1]
                        ysend[side, 1, p * 4 + m : p * 4 + m + 1, :] = value
                        mine = sum_moment(own, m)
                        mown[side, p * 4 + m : p * 4 + m + 1, :] = (
                            jnp.zeros((1, 128), jnp.float32) if mine is None else mine[7 - row : 8 - row]
                        )
                for q, names, source, at in ((0, GO_RIGHT, 1, 0), (1, GO_LEFT, 0, 4)):
                    q = q + (0 if side == UP else 2)
                    flat_set = [(i, moved[i][source]) for i in names if VEL[i][1] == 0]
                    steep_set = [(i, moved[i][source]) for i in names if VEL[i][1] == sign]
                    for m in range(4):
                        flat = sum_moment(flat_set, m)
                        steep = sum_moment(steep_set, m)
                        value = 0.0
                        if flat is not None:
                            value = flat[row : row + 1]
                        if steep is not None:
                            value = value + steep[inner : inner + 1]
                        dsend[step, q, at + m : at + m + 1, :] = value
        for q, where in enumerate(diagonals):
            sent.append(launch(dsend.at[step, q], drecv.at[step, q], d_send.at[step, q], d_recv.at[step, q], where))
        for side, where in ((UP, (s, t_next)), (DOWN, (s, t_prev))):
            if step < STEPS - 1:
                source, target = ysend.at[side], yrecv.at[side]
            else:
                source, target = ylast.at[side], ylast_recv.at[side]
            sent.append(launch(source, target, y_send.at[step, side], y_recv.at[step, side], where))
        return sent

    def sum_moment(members, m):
        if m == 0:
            return add_up((1, value) for i, value in members)
        return add_up((VEL[i][m - 1], value) for i, value in members)

    def stream(step, moved):
        new = []
        for i in range(19):
            cx, cy, unused = VEL[i]
            planes = []
            for p in range(2):
                source = p - cx
                if source in (0, 1):
                    tile = moved[i][source]
                elif cx == 1:
                    tile = xrecv[step, 0, GO_RIGHT.index(i)]
                else:
                    tile = xrecv[step, 1, GO_LEFT.index(i)]
                if cy != 0:
                    side = UP if cy == 1 else DOWN
                    rows = ROWS_UP if cy == 1 else ROWS_DOWN
                    if source in (0, 1):
                        at = rows.index((i, source, p))
                        edge = got_row(step, side, at)
                    else:
                        q = (0 if cx == 1 else 1) + (0 if cy == 1 else 2)
                        at = 4 if cx == 1 else 0
                        edge = drecv[step, q, at : at + 1, :]
                    tile = jnp.where(row_of == (0 if cy == 1 else 7), edge, pltpu.roll(tile, cy % 8, 0))
                planes.append(tile)
            new.append(jnp.stack(planes))
        return new

    def edge_moments(step, side):
        low = row_of < 4
        total = yrecv[side, 1] + mown[side]
        q = 0 if side == UP else 2
        total = total + jnp.where(low, drecv[step, q], drecv[step, q + 1])
        sign = 1 if side == UP else -1
        row = 0 if side == UP else 7
        i = 9 if side == UP else 7
        left = xrecv[step, 0, GO_RIGHT.index(i), row : row + 1, :]
        i = 8 if side == UP else 10
        right = xrecv[step, 1, GO_LEFT.index(i), row : row + 1, :]
        total = total + jnp.where((row_of == 0) | (row_of == 1), left, 0.0)
        total = total + jnp.where(row_of == 2, -sign * left, 0.0)
        total = total + jnp.where(row_of == 4, right, 0.0)
        total = total + jnp.where(row_of == 5, -right, 0.0)
        total = total + jnp.where(row_of == 6, -sign * right, 0.0)
        return total

    def edge_velocity(total):
        values = []
        for p in range(2):
            inv = 1.0 / total[p * 4 : p * 4 + 1]
            values.append(total[p * 4 + 1 : p * 4 + 4] * inv)
        return values

    solid = solid_ref[...]

    def others(action):
        for row in range(run):
            for offset in others_x:
                action(row * columns + column(offset))
            pl.when(row != z)(functools.partial(action, row * columns + x))

    def finish_gather():
        halo_copy(UP).wait_send()
        halo_copy(DOWN).wait_send()
        pl.when(z == h)(lambda: wrap_on().wait_send())
        for row in range(run):

            @pl.when((z >= h) | (row < h))
            def _():
                for offset in others_x:
                    tile_copy(t_next, row * columns + column(offset)).wait_send()
                pl.when(row != z)(lambda: tile_copy(t_next, row * columns + x).wait_send())

        pl.when(lower)(lambda: level_copy(z, t_next, z).wait_send())
        for k in range(h):
            pl.when((z >= h) & (k != z - h))(lambda: level_copy(0, t_next, k).wait_send())

    g = marker_pass(0)
    moved = deep(collide(f, rho, mom, g, solid))
    for q in range(6):
        pl.when(heights[q] > level)(functools.partial(await_ready, q))
    first_rims = exchange(0, moved)
    finish_gather()
    for copy in first_rims:
        copy.wait_recv()
    f = stream(0, moved)
    low = edge_velocity(edge_moments(0, UP))
    high = edge_velocity(edge_moments(0, DOWN))
    for p in range(2):
        hbuf[p, 0:3, :] = low[p]
        hbuf[p, 3:6, :] = high[p]
    rho, mom = moments(f)
    inv = 1.0 / rho
    set_velocity([mom[d] * inv for d in range(3)])

    g = marker_pass(1)

    moved = deep(collide(f, rho, mom, g, solid))
    rims = exchange(1, moved)
    for row in range(run):
        for offset in others_x:
            return_copy(column(offset) * run + row, row * columns + column(offset)).start()
        pl.when(row != z)(lambda: return_copy(x * run + row, row * columns + x).start())
    urecv[own] = uret[own]
    others(return_wait)
    vel = [urecv[k] for k in range(n_trans)]
    while len(vel) > 1:
        vel = [vel[k] + vel[k + 1] for k in range(0, len(vel), 2)]
    force_ref[...] = gath[own, 7:8, :] * (gath[own, 4:7, :] - vel[0][0:3])
    for copy in first_rims:
        copy.wait_send()
    others(lambda slot: return_copy(t_next, slot).wait_send())
    for copy in rims:
        copy.wait_recv()
    f = stream(1, moved)
    for i in range(19):
        out_ref[i] = f[i]
    for copy in rims:
        copy.wait_send()


def per_device(n_stream, n_trans, populations, solid, support, fractions, target, area):
    columns = 4 if n_trans % 32 == 0 else 2
    run = n_trans // columns
    dma = pltpu.SemaphoreType.DMA
    f32 = jnp.float32
    vmem = pl.BlockSpec(memory_space=pltpu.VMEM)
    markers = support.shape[0]
    return pl.pallas_call(
        functools.partial(kernel, n_stream, n_trans, columns),
        out_shape=(
            jax.ShapeDtypeStruct(populations.shape, f32),
            jax.ShapeDtypeStruct((3, markers), f32),
        ),
        in_specs=[pl.BlockSpec(memory_space=pltpu.MemorySpace.HBM)] * 6,
        out_specs=(vmem, vmem),
        scratch_shapes=[
            pltpu.VMEM(populations.shape, f32),
            pltpu.VMEM(solid.shape, jnp.int32),
            pltpu.VMEM((1, markers), jnp.int32),
            pltpu.VMEM((3, markers), f32),
            pltpu.VMEM((3, markers), f32),
            pltpu.VMEM((1, markers), f32),
            pltpu.VMEM((n_trans, 8, 128), f32),
            pltpu.VMEM((columns, 128, run * 128), jnp.bfloat16),
            pltpu.VMEM((128, 256), jnp.bfloat16),
            pltpu.VMEM((2, 8, 128), f32),
            pltpu.VMEM((2, 8, 128), f32),
            pltpu.VMEM((8, 128), f32),
            pltpu.VMEM((2, 8, 128), f32),
            pltpu.VMEM((2, 2, 5, 8, 128), f32),
            pltpu.VMEM((2, 2, 5, 8, 128), f32),
            pltpu.VMEM((2, 2, 8, 128), f32),
            pltpu.VMEM((2, 2, 8, 128), f32),
            pltpu.VMEM((2, 8, 128), f32),
            pltpu.VMEM((2, 8, 128), f32),
            pltpu.VMEM((2, 8, 128), f32),
            pltpu.VMEM((2, 4, 8, 128), f32),
            pltpu.VMEM((2, 4, 8, 128), f32),
            pltpu.VMEM((n_trans, 3, 128), f32),
            pltpu.VMEM((n_trans, 3, 128), f32),
            dma((6,)),
            pltpu.SemaphoreType.REGULAR((8,)),
            dma,
            dma,
            dma((run,)),
            dma((run,)),
            dma((n_trans,)),
            dma((n_trans,)),
            dma((2,)),
            dma((2,)),
            dma((2, 2)),
            dma((2, 2)),
            dma((2, 2)),
            dma((2, 2)),
            dma((2, 4)),
            dma((2, 4)),
            dma((n_trans,)),
            dma((n_trans,)),
        ],
        compiler_params=pltpu.CompilerParams(
            collective_id=0, has_side_effects=True, vmem_limit_bytes=56 * 1024 * 1024
        ),
        name="tract",
    )(
        populations,
        solid,
        support.reshape(1, markers),
        fractions,
        target,
        area.reshape(1, markers),
    )


def solution(mesh):
    placed = (
        P(None, "stream", "trans", None),
        P("stream", "trans", None),
        P(("stream", "trans")),
        P(None, ("stream", "trans")),
        P(None, ("stream", "trans")),
        P(("stream", "trans")),
    )
    return jax.shard_map(
        functools.partial(per_device, mesh.shape["stream"], mesh.shape["trans"]),
        mesh=mesh,
        in_specs=placed,
        out_specs=(P(None, "stream", "trans", None), P(None, ("stream", "trans"))),
        check_vma=False,
    )
```

```python
import functools
import math

import jax
import jax.numpy as jnp
from jax import lax
from jax.experimental import pallas as pl
from jax.experimental.pallas import tpu as pltpu
from jax.sharding import PartitionSpec as P

STEPS = 2
VEL = (
    (0, 0, 0),
    (1, 0, 0),
    (-1, 0, 0),
    (0, 1, 0),
    (0, -1, 0),
    (0, 0, 1),
    (0, 0, -1),
    (1, 1, 0),
    (-1, -1, 0),
    (1, -1, 0),
    (-1, 1, 0),
    (1, 0, 1),
    (-1, 0, -1),
    (1, 0, -1),
    (-1, 0, 1),
    (0, 1, 1),
    (0, -1, -1),
    (0, 1, -1),
    (0, -1, 1),
)
WEIGHT = (1.0 / 3.0,) + (1.0 / 18.0,) * 6 + (1.0 / 36.0,) * 12
OPP = (0, 2, 1, 4, 3, 6, 5, 8, 7, 10, 9, 12, 11, 14, 13, 16, 15, 18, 17)
TAU_BASE = 0.8
SMAG = 0.17
MESH = pl.DeviceIdType.MESH
UP = 0
DOWN = 1
GO_RIGHT = (1, 7, 9, 11, 13)
GO_LEFT = (2, 8, 10, 12, 14)
ROWS_UP = ((3, 0, 0), (3, 1, 1), (15, 0, 0), (15, 1, 1), (17, 0, 0), (17, 1, 1), (7, 0, 1), (10, 1, 0))
ROWS_DOWN = ((4, 0, 0), (4, 1, 1), (16, 0, 0), (16, 1, 1), (18, 0, 0), (18, 1, 1), (8, 1, 0), (9, 0, 1))


def add_up(terms):
    total = None
    for sign, value in terms:
        if sign == 0:
            continue
        if total is None:
            total = value if sign > 0 else -value
        else:
            total = total + value if sign > 0 else total - value
    return total


def combine(factors, values):
    total = add_up(zip(factors, values))
    return 0.0 if total is None else total


def moments(f):
    rho = add_up((1, f[i]) for i in range(19))
    mom = [add_up((VEL[i][d], f[i]) for i in range(19)) for d in range(3)]
    return rho, mom


def collide(f, rho, mom, g, solid):
    inv_rho = 1.0 / rho
    u = [(mom[d] + 0.5 * g[d]) * inv_rho for d in range(3)]
    square = u[0] * u[0] + u[1] * u[1] + u[2] * u[2]
    ug = u[0] * g[0] + u[1] * g[1] + u[2] * g[2]
    base = 1.0 - 1.5 * square
    proj = [combine(VEL[i], u) for i in range(19)]
    neq = []
    for i in range(19):
        feq = WEIGHT[i] * rho * (base + 3.0 * proj[i] + 4.5 * proj[i] * proj[i])
        neq.append(f[i] - feq)
    mag2 = 0.0
    for a, b in ((0, 0), (1, 1), (2, 2), (0, 1), (0, 2), (1, 2)):
        comp = combine([VEL[i][a] * VEL[i][b] for i in range(19)], neq)
        mag2 = mag2 + (1.0 if a == b else 2.0) * comp * comp
    mag = jnp.sqrt(mag2)
    tau = 0.5 * (
        TAU_BASE + jnp.sqrt(TAU_BASE * TAU_BASE + 18.0 * math.sqrt(2.0) * SMAG * SMAG * mag * inv_rho)
    )
    inv_tau = 1.0 / tau
    share = 1.0 - 0.5 * inv_tau
    is_solid = solid == 1
    out = []
    for i in range(19):
        cg = combine(VEL[i], g)
        source = share * (WEIGHT[i] * (3.0 * (cg - ug) + 9.0 * proj[i] * cg))
        out.append(jnp.where(is_solid, f[OPP[i]], f[i] - neq[i] * inv_tau + source))
    return out


def split(x, axis):
    hi = x.astype(jnp.bfloat16)
    lo = (x - hi.astype(jnp.float32)).astype(jnp.bfloat16)
    return jnp.concatenate([hi, lo], axis=axis)


def kernel(
    n_stream,
    n_trans,
    columns,
    pop_hbm,
    solid_hbm,
    support_hbm,
    frac_hbm,
    target_hbm,
    area_hbm,
    out_ref,
    force_ref,
    pop_ref,
    solid_ref,
    support_ref,
    frac_ref,
    target_ref,
    area_ref,
    gath,
    onehot,
    vs,
    htile,
    hrecv,
    wrap,
    hbuf,
    xsend,
    xrecv,
    ysend,
    yrecv,
    ylast,
    ylast_recv,
    mown,
    dsend,
    drecv,
    uret,
    urecv,
    in_sem,
    ready,
    w_send,
    w_recv,
    l_send,
    l_recv,
    g_send,
    g_recv,
    h_send,
    h_recv,
    x_send,
    x_recv,
    y_send,
    y_recv,
    d_send,
    d_recv,
    u_send,
    u_recv,
):
    s = lax.axis_index("stream")
    t = lax.axis_index("trans")
    s_next = lax.rem(s + 1, n_stream)
    s_prev = lax.rem(s + n_stream - 1, n_stream)
    t_next = lax.rem(t + 1, n_trans)
    t_prev = lax.rem(t + n_trans - 1, n_trans)
    diagonals = ((s_next, t_next), (s_prev, t_next), (s_next, t_prev), (s_prev, t_prev))

    run = n_trans // columns
    x = t // run
    z = lax.rem(t, run)
    own = z * columns + x
    h = run // 2
    lower = z < h
    half = max(n_stream // 2, 1)
    partners = ((s_next, t), (s_prev, t)) + diagonals + ((s, t_next), (s, t_prev))
    back = (1, 0, 5, 4, 3, 2, 7, 6)

    def height(where):
        return (where[0] // half) * run + lax.rem(where[1], run)

    heights = [height(where) for where in partners]
    level = height((s, t))
    others_x = (2, 1, 3) if columns == 4 else tuple(range(1, columns))

    def column(offset):
        return lax.rem(x + offset, columns)

    loads = [
        pltpu.make_async_copy(source, target, in_sem.at[k])
        for k, (source, target) in enumerate(
            (
                (pop_hbm, pop_ref),
                (support_hbm, support_ref),
                (frac_hbm, frac_ref),
                (target_hbm, target_ref),
                (area_hbm, area_ref),
                (solid_hbm, solid_ref),
            )
        )
    ]
    for load in loads:
        load.start()
    barrier = pltpu.get_barrier_semaphore()

    def greet(where):
        pl.semaphore_signal(barrier, inc=1, device_id=where, device_id_type=MESH)

    expected = jnp.where(lower, h * columns, n_trans) - 1
    for row in range(run):

        @pl.when(lower | (row >= h))
        def _():
            for offset in others_x:
                greet((s, column(offset) * run + row))
            pl.when(row != z)(lambda: greet((s, x * run + row)))

    pl.when(z >= h)(lambda: greet((s, t - h)))
    expected = expected + lower.astype(jnp.int32)
    if h > 1:
        pl.when(z == h)(lambda: greet((s, t_prev)))
        expected = expected + (z == h - 1).astype(jnp.int32)
    pl.when(z == h)(lambda: greet((s, column(1) * run)))
    expected = expected + (z == 0).astype(jnp.int32)
    for where, height_there in zip(partners[:6], heights[:6]):
        pl.when(height_there >= level)(functools.partial(greet, where))
        expected = expected + (height_there <= level).astype(jnp.int32)

    for load in loads[1:5]:
        load.wait()

    gath[own, 0:1, :] = support_ref[...].astype(jnp.float32)
    gath[own, 1:4, :] = frac_ref[...]
    gath[own, 4:7, :] = target_ref[...]
    gath[own, 7:8, :] = area_ref[...]

    loads[0].wait()
    loads[5].wait()
    f = [pop_ref[i] for i in range(19)]
    rho, mom = moments(f)
    inv = 1.0 / rho
    ustar = [mom[d] * inv for d in range(3)]
    htile[...] = jnp.zeros_like(htile)
    for p in range(2):
        for d in range(3):
            htile[UP, p * 4 + d : p * 4 + d + 1, :] = ustar[d][p, 7:8, :]
            htile[DOWN, p * 4 + d : p * 4 + d + 1, :] = ustar[d][p, 0:1, :]

    pl.semaphore_wait(barrier, expected)

    def answer(q):
        pl.semaphore_signal(ready.at[back[q]], inc=1, device_id=partners[q], device_id_type=MESH)

    def await_ready(q):
        pl.semaphore_wait(ready.at[q], 1)

    def remote(src, dst, send, recv, where):
        return pltpu.make_async_remote_copy(
            src_ref=src, dst_ref=dst, send_sem=send, recv_sem=recv, device_id=where, device_id_type=MESH
        )

    def launch(*args):
        copy = remote(*args)
        copy.start()
        return copy

    def tile_copy(where, slot):
        return remote(gath.at[own], gath.at[own], g_send.at[slot], g_recv.at[own], (s, where))

    def tile_wait(slot):
        remote(gath.at[own], gath.at[slot], g_send.at[slot], g_recv.at[slot], (s, t_next)).wait_recv()

    def level_copy(row, where, k):
        part = gath.at[pl.ds(row * columns, columns)]
        return remote(part, part, l_send.at[k], l_recv.at[row], (s, where))

    def halo_copy(side):
        where = (s, t_next if side == UP else t_prev)
        return remote(htile.at[side], hrecv.at[side], h_send.at[side], h_recv.at[side], where)

    def wrap_copy():
        return remote(
            htile.at[DOWN], wrap, h_send.at[DOWN], w_recv, (s, column(columns - 1) * run + h)
        )

    def wrap_on():
        return remote(wrap, hrecv.at[DOWN], w_send, h_recv.at[DOWN], (s, x * run + run - 1))

    halo_copy(UP).start()
    pl.when(z > 0)(lambda: halo_copy(DOWN).start())
    pl.when(z == 0)(lambda: wrap_copy().start())

    for row in range(run):

        @pl.when((z >= h) | (row < h))
        def _():
            for offset in others_x:
                tile_copy(column(offset) * run + row, row * columns + column(offset)).start()
            pl.when(row != z)(lambda: tile_copy(x * run + row, row * columns + x).start())

    @pl.when(lower)
    def _():
        for offset in others_x:
            tile_wait(z * columns + column(offset))
        level_copy(z, t + h, z).start()

    for row in range(h):

        @pl.when(row == z - h)
        def _():
            level_copy(row, t_next, row).wait_recv()
            for k in range(h):
                if k != row:
                    level_copy(row, x * run + h + k, k).start()

    @pl.when(z == h)
    def _():
        wrap_copy().wait_recv()
        wrap_on().start()

    for q in range(6):
        pl.when(heights[q] < level)(functools.partial(answer, q))
    halo_copy(UP).wait_recv()
    halo_copy(DOWN).wait_recv()

    hbuf[...] = jnp.zeros_like(hbuf)

    def set_halo(lo, hi):
        for p in range(2):
            hbuf[p, 0:3, :] = lo[p * 4 : p * 4 + 3, :]
            hbuf[p, 3:6, :] = hi[p * 4 : p * 4 + 3, :]

    def set_velocity(ustar):
        rows = []
        for shift in (0, 1):
            for d in range(3):
                for p in range(2):
                    x = ustar[d][p]
                    rows.append(pltpu.roll(x, 127, 1) if shift else x)
        for shift in (0, 1):
            for p in range(2):
                x = hbuf[p]
                rows.append(pltpu.roll(x, 127, 1) if shift else x)
        vs[...] = split(jnp.concatenate(rows, axis=0), 1)

    set_halo(hrecv[UP], hrecv[DOWN])
    set_velocity(ustar)

    tiles = n_trans // columns
    width = tiles * 128
    rows_of = tiles // columns
    first_row = (t * 8).astype(jnp.float32)

    def return_copy(where, slot):
        return remote(uret.at[slot], urecv.at[own], u_send.at[slot], u_recv.at[own], (s, where))

    def return_wait(slot):
        remote(uret.at[slot], urecv.at[slot], u_send.at[slot], u_recv.at[slot], (s, t_next)).wait_recv()

    def marker_pass(step):
        def chunk(j):
            first = j * tiles
            rows = range(j * rows_of, (j + 1) * rows_of)
            if step == 0:
                for row in rows:
                    if row < h:

                        @pl.when(lower & (row != z))
                        def _():
                            for offset in range(columns):
                                tile_wait(row * columns + offset)

                        pl.when((z >= h) & (row != z - h))(
                            lambda: level_copy(row, t_next, 0).wait_recv()
                        )
                    else:
                        for offset in others_x:
                            tile_wait(row * columns + column(offset))
                        pl.when(row != z)(lambda: tile_wait(row * columns + x))

            tile = jnp.concatenate([gath[first + i] for i in range(tiles)], axis=1)
            fx, fy, fz = tile[1:2], tile[2:3], tile[3:4]
            b = jnp.floor(tile[0:1] * (1.0 / 128.0))
            if step == 0:
                e = tile[0:1] - 128.0 * b
                depth = lax.broadcasted_iota(jnp.int32, (128, width), 0).astype(jnp.float32)
                pick = jnp.where(depth == e, 1.0, 0.0).astype(jnp.bfloat16)
                onehot[j] = pick
            else:
                pick = onehot[j]
            r = lax.dot_general(
                vs[...],
                jnp.concatenate([pick, pick], axis=0),
                (((1,), (0,)), ((), ())),
                preferred_element_type=jnp.float32,
            )
            gx, gy, gz = 1.0 - fx, 1.0 - fy, 1.0 - fz
            local = lax.broadcasted_iota(jnp.int32, (8, width), 0).astype(jnp.float32)
            rel = b - first_row
            wy = jnp.where(local == rel, gy, 0.0) + jnp.where(local == rel + 1.0, fy, 0.0)
            wh = jnp.where(
                local < 3.0, jnp.where(rel == -1.0, gy, 0.0), jnp.where(rel == 7.0, fy, 0.0)
            )

            def lerp(at):
                planes = []
                for p in range(2):
                    low, high = at(0, p), at(1, p)
                    planes.append(low * gz + high * fz)
                return planes[0] * gx + planes[1] * fx

            edge = wh * lerp(lambda shift, p: r[(12 + shift * 2 + p) * 8 : (12 + shift * 2 + p) * 8 + 8])
            vel = []
            for d in range(3):
                own = lerp(
                    lambda shift, p: r[((shift * 3 + d) * 2 + p) * 8 : ((shift * 3 + d) * 2 + p) * 8 + 8]
                )
                vel.append(
                    jnp.sum(wy * own, axis=0, keepdims=True) + edge[d : d + 1] + edge[3 + d : 4 + d]
                )
            if step == STEPS - 1:
                mine = (rel >= 0.0) & (rel <= 7.0)
                for d in range(3):
                    back_to = jnp.where(mine, vel[d], 0.0)
                    for i in range(tiles):
                        uret[first + i, d : d + 1, :] = back_to[:, i * 128 : i * 128 + 128]
            spread = []
            wyz = [wy * gz, wy * fz]
            wx = (gx, fx)
            pushes = [tile[7:8] * (tile[4 + d : 5 + d] - vel[d]) for d in range(3)]
            for shift in (0, 1):
                for d in range(3):
                    for p in range(2):
                        spread.append(wyz[shift] * (pushes[d] * wx[p]))
            return lax.dot_general(
                split(jnp.concatenate(spread, axis=0), 0),
                pick,
                (((1,), (1,)), ((), ())),
                preferred_element_type=jnp.float32,
            )

        total = None
        for j in range(columns):
            part = chunk(j)
            total = part if total is None else total + part
        total = total[0:96] + total[96:192]
        g = []
        for d in range(3):
            planes = []
            for p in range(2):
                low = total[(d * 2 + p) * 8 : (d * 2 + p) * 8 + 8]
                high = total[((3 + d) * 2 + p) * 8 : ((3 + d) * 2 + p) * 8 + 8]
                planes.append(low + pltpu.roll(high, 1, 1))
            g.append(jnp.stack(planes))
        return g

    row_of = lax.broadcasted_iota(jnp.int32, (8, 128), 0)

    def deep(post):
        return [
            [
                pltpu.roll(post[i][p], VEL[i][2] % 128, 1) if VEL[i][2] else post[i][p]
                for p in range(2)
            ]
            for i in range(19)
        ]

    def put_row(step, side, at, value):
        if step < STEPS - 1:
            ysend[side, 0, at : at + 1, :] = value
        else:
            ylast[side, at : at + 1, :] = value

    def got_row(step, side, at):
        if step < STEPS - 1:
            return yrecv[side, 0, at : at + 1, :]
        return ylast_recv[side, at : at + 1, :]

    def exchange(step, moved):
        sent = []
        for q, i in enumerate(GO_RIGHT):
            xsend[step, 0, q] = moved[i][1]
        for q, i in enumerate(GO_LEFT):
            xsend[step, 1, q] = moved[i][0]
        sent.append(launch(xsend.at[step, 0], xrecv.at[step, 0], x_send.at[step, 0], x_recv.at[step, 0], (s_next, t)))
        sent.append(launch(xsend.at[step, 1], xrecv.at[step, 1], x_send.at[step, 1], x_recv.at[step, 1], (s_prev, t)))
        for q, (i, source, unused) in enumerate(ROWS_UP):
            put_row(step, UP, q, moved[i][source][7:8])
        for q, (i, source, unused) in enumerate(ROWS_DOWN):
            put_row(step, DOWN, q, moved[i][source][0:1])
        corner = ((7, 1, 7), (10, 0, 7), (9, 1, 0), (8, 0, 0))
        for q, (i, source, row) in enumerate(corner):
            dsend[step, q] = jnp.broadcast_to(moved[i][source][row : row + 1], (8, 128))
        if step < STEPS - 1:
            for side, sign, row in ((UP, 1, 7), (DOWN, -1, 0)):
                inner = row - sign
                for p in range(2):
                    level = {0: [], sign: []}
                    own = []
                    for i in range(19):
                        source = p - VEL[i][0]
                        if source not in (0, 1):
                            continue
                        if VEL[i][1] in level:
                            level[VEL[i][1]].append((i, moved[i][source]))
                        else:
                            own.append((i, moved[i][source]))
                    for m in range(4):
                        flat = sum_moment(level[0], m)
                        steep = sum_moment(level[sign], m)
                        value = 0.0
                        if flat is not None:
                            value = flat[row : row + 1]
                        if steep is not None:
                            value = value + steep[inner : inner + 1]
                        ysend[side, 1, p * 4 + m : p * 4 + m + 1, :] = value
                        mine = sum_moment(own, m)
                        mown[side, p * 4 + m : p * 4 + m + 1, :] = (
                            jnp.zeros((1, 128), jnp.float32) if mine is None else mine[7 - row : 8 - row]
                        )
                for q, names, source, at in ((0, GO_RIGHT, 1, 0), (1, GO_LEFT, 0, 4)):
                    q = q + (0 if side == UP else 2)
                    flat_set = [(i, moved[i][source]) for i in names if VEL[i][1] == 0]
                    steep_set = [(i, moved[i][source]) for i in names if VEL[i][1] == sign]
                    for m in range(4):
                        flat = sum_moment(flat_set, m)
                        steep = sum_moment(steep_set, m)
                        value = 0.0
                        if flat is not None:
                            value = flat[row : row + 1]
                        if steep is not None:
                            value = value + steep[inner : inner + 1]
                        dsend[step, q, at + m : at + m + 1, :] = value
        for q, where in enumerate(diagonals):
            sent.append(launch(dsend.at[step, q], drecv.at[step, q], d_send.at[step, q], d_recv.at[step, q], where))
        for side, where in ((UP, (s, t_next)), (DOWN, (s, t_prev))):
            if step < STEPS - 1:
                source, target = ysend.at[side], yrecv.at[side]
            else:
                source, target = ylast.at[side], ylast_recv.at[side]
            sent.append(launch(source, target, y_send.at[step, side], y_recv.at[step, side], where))
        return sent

    def sum_moment(members, m):
        if m == 0:
            return add_up((1, value) for i, value in members)
        return add_up((VEL[i][m - 1], value) for i, value in members)

    def stream(step, moved):
        new = []
        for i in range(19):
            cx, cy, unused = VEL[i]
            planes = []
            for p in range(2):
                source = p - cx
                if source in (0, 1):
                    tile = moved[i][source]
                elif cx == 1:
                    tile = xrecv[step, 0, GO_RIGHT.index(i)]
                else:
                    tile = xrecv[step, 1, GO_LEFT.index(i)]
                if cy != 0:
                    side = UP if cy == 1 else DOWN
                    rows = ROWS_UP if cy == 1 else ROWS_DOWN
                    if source in (0, 1):
                        at = rows.index((i, source, p))
                        edge = got_row(step, side, at)
                    else:
                        q = (0 if cx == 1 else 1) + (0 if cy == 1 else 2)
                        at = 4 if cx == 1 else 0
                        edge = drecv[step, q, at : at + 1, :]
                    tile = jnp.where(row_of == (0 if cy == 1 else 7), edge, pltpu.roll(tile, cy % 8, 0))
                planes.append(tile)
            new.append(jnp.stack(planes))
        return new

    def edge_moments(step, side):
        low = row_of < 4
        total = yrecv[side, 1] + mown[side]
        q = 0 if side == UP else 2
        total = total + jnp.where(low, drecv[step, q], drecv[step, q + 1])
        sign = 1 if side == UP else -1
        row = 0 if side == UP else 7
        i = 9 if side == UP else 7
        left = xrecv[step, 0, GO_RIGHT.index(i), row : row + 1, :]
        i = 8 if side == UP else 10
        right = xrecv[step, 1, GO_LEFT.index(i), row : row + 1, :]
        total = total + jnp.where((row_of == 0) | (row_of == 1), left, 0.0)
        total = total + jnp.where(row_of == 2, -sign * left, 0.0)
        total = total + jnp.where(row_of == 4, right, 0.0)
        total = total + jnp.where(row_of == 5, -right, 0.0)
        total = total + jnp.where(row_of == 6, -sign * right, 0.0)
        return total

    def edge_velocity(total):
        values = []
        for p in range(2):
            inv = 1.0 / total[p * 4 : p * 4 + 1]
            values.append(total[p * 4 + 1 : p * 4 + 4] * inv)
        return values

    solid = solid_ref[...]

    def others(action):
        for row in range(run):
            for offset in others_x:
                action(row * columns + column(offset))
            pl.when(row != z)(functools.partial(action, row * columns + x))

    def finish_gather():
        halo_copy(UP).wait_send()
        halo_copy(DOWN).wait_send()
        pl.when(z == h)(lambda: wrap_on().wait_send())
        for row in range(run):

            @pl.when((z >= h) | (row < h))
            def _():
                for offset in others_x:
                    tile_copy(t_next, row * columns + column(offset)).wait_send()
                pl.when(row != z)(lambda: tile_copy(t_next, row * columns + x).wait_send())

        pl.when(lower)(lambda: level_copy(z, t_next, z).wait_send())
        for k in range(h):
            pl.when((z >= h) & (k != z - h))(lambda: level_copy(0, t_next, k).wait_send())

    g = marker_pass(0)
    moved = deep(collide(f, rho, mom, g, solid))
    for q in range(6):
        pl.when(heights[q] > level)(functools.partial(await_ready, q))
    first_rims = exchange(0, moved)
    finish_gather()
    for copy in first_rims:
        copy.wait_recv()
    f = stream(0, moved)
    low = edge_velocity(edge_moments(0, UP))
    high = edge_velocity(edge_moments(0, DOWN))
    for p in range(2):
        hbuf[p, 0:3, :] = low[p]
        hbuf[p, 3:6, :] = high[p]
    rho, mom = moments(f)
    inv = 1.0 / rho
    set_velocity([mom[d] * inv for d in range(3)])

    g = marker_pass(1)

    moved = deep(collide(f, rho, mom, g, solid))
    rims = exchange(1, moved)
    for row in range(run):
        for offset in others_x:
            return_copy(column(offset) * run + row, row * columns + column(offset)).start()
        pl.when(row != z)(lambda: return_copy(x * run + row, row * columns + x).start())
    urecv[own] = uret[own]
    others(return_wait)
    vel = [urecv[k] for k in range(n_trans)]
    while len(vel) > 1:
        vel = [vel[k] + vel[k + 1] for k in range(0, len(vel), 2)]
    force_ref[...] = gath[own, 7:8, :] * (gath[own, 4:7, :] - vel[0][0:3])
    for copy in first_rims:
        copy.wait_send()
    others(lambda slot: return_copy(t_next, slot).wait_send())
    for copy in rims:
        copy.wait_recv()
    f = stream(1, moved)
    for i in range(19):
        out_ref[i] = f[i]
    for copy in rims:
        copy.wait_send()


def per_device(n_stream, n_trans, populations, solid, support, fractions, target, area):
    columns = 4 if n_trans % 32 == 0 else 2
    run = n_trans // columns
    dma = pltpu.SemaphoreType.DMA
    f32 = jnp.float32
    vmem = pl.BlockSpec(memory_space=pltpu.VMEM)
    markers = support.shape[0]
    return pl.pallas_call(
        functools.partial(kernel, n_stream, n_trans, columns),
        out_shape=(
            jax.ShapeDtypeStruct(populations.shape, f32),
            jax.ShapeDtypeStruct((3, markers), f32),
        ),
        in_specs=[pl.BlockSpec(memory_space=pltpu.MemorySpace.HBM)] * 6,
        out_specs=(vmem, vmem),
        scratch_shapes=[
            pltpu.VMEM(populations.shape, f32),
            pltpu.VMEM(solid.shape, jnp.int32),
            pltpu.VMEM((1, markers), jnp.int32),
            pltpu.VMEM((3, markers), f32),
            pltpu.VMEM((3, markers), f32),
            pltpu.VMEM((1, markers), f32),
            pltpu.VMEM((n_trans, 8, 128), f32),
            pltpu.VMEM((columns, 128, run * 128), jnp.bfloat16),
            pltpu.VMEM((128, 256), jnp.bfloat16),
            pltpu.VMEM((2, 8, 128), f32),
            pltpu.VMEM((2, 8, 128), f32),
            pltpu.VMEM((8, 128), f32),
            pltpu.VMEM((2, 8, 128), f32),
            pltpu.VMEM((2, 2, 5, 8, 128), f32),
            pltpu.VMEM((2, 2, 5, 8, 128), f32),
            pltpu.VMEM((2, 2, 8, 128), f32),
            pltpu.VMEM((2, 2, 8, 128), f32),
            pltpu.VMEM((2, 8, 128), f32),
            pltpu.VMEM((2, 8, 128), f32),
            pltpu.VMEM((2, 8, 128), f32),
            pltpu.VMEM((2, 4, 8, 128), f32),
            pltpu.VMEM((2, 4, 8, 128), f32),
            pltpu.VMEM((n_trans, 3, 128), f32),
            pltpu.VMEM((n_trans, 3, 128), f32),
            dma((6,)),
            pltpu.SemaphoreType.REGULAR((8,)),
            dma,
            dma,
            dma((run,)),
            dma((run,)),
            dma((n_trans,)),
            dma((n_trans,)),
            dma((2,)),
            dma((2,)),
            dma((2, 2)),
            dma((2, 2)),
            dma((2, 2)),
            dma((2, 2)),
            dma((2, 4)),
            dma((2, 4)),
            dma((n_trans,)),
            dma((n_trans,)),
        ],
        compiler_params=pltpu.CompilerParams(
            collective_id=0, has_side_effects=True, vmem_limit_bytes=56 * 1024 * 1024
        ),
        name="tract",
    )(
        populations,
        solid,
        support.reshape(1, markers),
        fractions,
        target,
        area.reshape(1, markers),
    )


def solution(mesh):
    placed = (
        P(None, "stream", "trans", None),
        P("stream", "trans", None),
        P(("stream", "trans")),
        P(None, ("stream", "trans")),
        P(None, ("stream", "trans")),
        P(("stream", "trans")),
    )
    return jax.shard_map(
        functools.partial(per_device, mesh.shape["stream"], mesh.shape["trans"]),
        mesh=mesh,
        in_specs=placed,
        out_specs=(P(None, "stream", "trans", None), P(None, ("stream", "trans"))),
        check_vma=False,
    )
```

```python
import functools
import math

import jax
import jax.numpy as jnp
from jax import lax
from jax.experimental import pallas as pl
from jax.experimental.pallas import tpu as pltpu
from jax.sharding import PartitionSpec as P

STEPS = 2
VEL = (
    (0, 0, 0),
    (1, 0, 0),
    (-1, 0, 0),
    (0, 1, 0),
    (0, -1, 0),
    (0, 0, 1),
    (0, 0, -1),
    (1, 1, 0),
    (-1, -1, 0),
    (1, -1, 0),
    (-1, 1, 0),
    (1, 0, 1),
    (-1, 0, -1),
    (1, 0, -1),
    (-1, 0, 1),
    (0, 1, 1),
    (0, -1, -1),
    (0, 1, -1),
    (0, -1, 1),
)
WEIGHT = (1.0 / 3.0,) + (1.0 / 18.0,) * 6 + (1.0 / 36.0,) * 12
OPP = (0, 2, 1, 4, 3, 6, 5, 8, 7, 10, 9, 12, 11, 14, 13, 16, 15, 18, 17)
TAU_BASE = 0.8
SMAG = 0.17
MESH = pl.DeviceIdType.MESH
UP = 0
DOWN = 1
GO_RIGHT = (1, 7, 9, 11, 13)
GO_LEFT = (2, 8, 10, 12, 14)
ROWS_UP = ((3, 0, 0), (3, 1, 1), (15, 0, 0), (15, 1, 1), (17, 0, 0), (17, 1, 1), (7, 0, 1), (10, 1, 0))
ROWS_DOWN = ((4, 0, 0), (4, 1, 1), (16, 0, 0), (16, 1, 1), (18, 0, 0), (18, 1, 1), (8, 1, 0), (9, 0, 1))


def add_up(terms):
    total = None
    for sign, value in terms:
        if sign == 0:
            continue
        if total is None:
            total = value if sign > 0 else -value
        else:
            total = total + value if sign > 0 else total - value
    return total


def combine(factors, values):
    total = add_up(zip(factors, values))
    return 0.0 if total is None else total


def moments(f):
    rho = add_up((1, f[i]) for i in range(19))
    mom = [add_up((VEL[i][d], f[i]) for i in range(19)) for d in range(3)]
    return rho, mom


def collide(f, rho, mom, g, solid):
    inv_rho = 1.0 / rho
    u = [(mom[d] + 0.5 * g[d]) * inv_rho for d in range(3)]
    square = u[0] * u[0] + u[1] * u[1] + u[2] * u[2]
    ug = u[0] * g[0] + u[1] * g[1] + u[2] * g[2]
    base = 1.0 - 1.5 * square
    proj = [combine(VEL[i], u) for i in range(19)]
    neq = []
    for i in range(19):
        feq = WEIGHT[i] * rho * (base + 3.0 * proj[i] + 4.5 * proj[i] * proj[i])
        neq.append(f[i] - feq)
    mag2 = 0.0
    for a, b in ((0, 0), (1, 1), (2, 2), (0, 1), (0, 2), (1, 2)):
        comp = combine([VEL[i][a] * VEL[i][b] for i in range(19)], neq)
        mag2 = mag2 + (1.0 if a == b else 2.0) * comp * comp
    mag = jnp.sqrt(mag2)
    tau = 0.5 * (
        TAU_BASE + jnp.sqrt(TAU_BASE * TAU_BASE + 18.0 * math.sqrt(2.0) * SMAG * SMAG * mag * inv_rho)
    )
    inv_tau = 1.0 / tau
    share = 1.0 - 0.5 * inv_tau
    is_solid = solid == 1
    out = []
    for i in range(19):
        cg = combine(VEL[i], g)
        source = share * (WEIGHT[i] * (3.0 * (cg - ug) + 9.0 * proj[i] * cg))
        out.append(jnp.where(is_solid, f[OPP[i]], f[i] - neq[i] * inv_tau + source))
    return out


def split(x, axis):
    hi = x.astype(jnp.bfloat16)
    lo = (x - hi.astype(jnp.float32)).astype(jnp.bfloat16)
    return jnp.concatenate([hi, lo], axis=axis)


def kernel(
    n_stream,
    n_trans,
    columns,
    pop_hbm,
    solid_hbm,
    support_hbm,
    frac_hbm,
    target_hbm,
    area_hbm,
    out_ref,
    force_ref,
    pop_ref,
    solid_ref,
    support_ref,
    frac_ref,
    target_ref,
    area_ref,
    gath,
    onehot,
    vs,
    htile,
    hrecv,
    wrap,
    hbuf,
    xsend,
    xrecv,
    ysend,
    yrecv,
    ylast,
    ylast_recv,
    mown,
    dsend,
    drecv,
    uret,
    urecv,
    in_sem,
    ready,
    w_send,
    w_recv,
    l_send,
    l_recv,
    g_send,
    g_recv,
    h_send,
    h_recv,
    x_send,
    x_recv,
    y_send,
    y_recv,
    d_send,
    d_recv,
    u_send,
    u_recv,
):
    s = lax.axis_index("stream")
    t = lax.axis_index("trans")
    s_next = lax.rem(s + 1, n_stream)
    s_prev = lax.rem(s + n_stream - 1, n_stream)
    t_next = lax.rem(t + 1, n_trans)
    t_prev = lax.rem(t + n_trans - 1, n_trans)
    diagonals = ((s_next, t_next), (s_prev, t_next), (s_next, t_prev), (s_prev, t_prev))

    run = n_trans // columns
    x = t // run
    z = lax.rem(t, run)
    own = z * columns + x
    h = run // 2
    lower = z < h
    half = max(n_stream // 2, 1)
    partners = ((s_next, t), (s_prev, t)) + diagonals + ((s, t_next), (s, t_prev))
    back = (1, 0, 5, 4, 3, 2, 7, 6)

    def height(where):
        return (where[0] // half) * run + lax.rem(where[1], run)

    heights = [height(where) for where in partners]
    level = height((s, t))
    others_x = (2, 1, 3) if columns == 4 else tuple(range(1, columns))

    def column(offset):
        return lax.rem(x + offset, columns)

    loads = [
        pltpu.make_async_copy(source, target, in_sem.at[k])
        for k, (source, target) in enumerate(
            (
                (pop_hbm, pop_ref),
                (support_hbm, support_ref),
                (frac_hbm, frac_ref),
                (target_hbm, target_ref),
                (area_hbm, area_ref),
                (solid_hbm, solid_ref),
            )
        )
    ]
    for load in loads:
        load.start()
    barrier = pltpu.get_barrier_semaphore()

    def greet(where):
        pl.semaphore_signal(barrier, inc=1, device_id=where, device_id_type=MESH)

    expected = jnp.where(lower, h * columns, n_trans) - 1
    for row in range(run):

        @pl.when(lower | (row >= h))
        def _():
            for offset in others_x:
                greet((s, column(offset) * run + row))
            pl.when(row != z)(lambda: greet((s, x * run + row)))

    pl.when(z >= h)(lambda: greet((s, t - h)))
    expected = expected + lower.astype(jnp.int32)
    if h > 1:
        pl.when(z == h)(lambda: greet((s, t_prev)))
        expected = expected + (z == h - 1).astype(jnp.int32)
    pl.when(z == h)(lambda: greet((s, column(1) * run)))
    expected = expected + (z == 0).astype(jnp.int32)
    for where, height_there in zip(partners[:6], heights[:6]):
        pl.when(height_there >= level)(functools.partial(greet, where))
        expected = expected + (height_there <= level).astype(jnp.int32)

    for load in loads[1:5]:
        load.wait()

    gath[own, 0:1, :] = support_ref[...].astype(jnp.float32)
    gath[own, 1:4, :] = frac_ref[...]
    gath[own, 4:7, :] = target_ref[...]
    gath[own, 7:8, :] = area_ref[...]

    loads[0].wait()
    loads[5].wait()
    f = [pop_ref[i] for i in range(19)]
    rho, mom = moments(f)
    inv = 1.0 / rho
    ustar = [mom[d] * inv for d in range(3)]
    htile[...] = jnp.zeros_like(htile)
    for p in range(2):
        for d in range(3):
            htile[UP, p * 4 + d : p * 4 + d + 1, :] = ustar[d][p, 7:8, :]
            htile[DOWN, p * 4 + d : p * 4 + d + 1, :] = ustar[d][p, 0:1, :]

    pl.semaphore_wait(barrier, expected)

    def answer(q):
        pl.semaphore_signal(ready.at[back[q]], inc=1, device_id=partners[q], device_id_type=MESH)

    def await_ready(q):
        pl.semaphore_wait(ready.at[q], 1)

    def remote(src, dst, send, recv, where):
        return pltpu.make_async_remote_copy(
            src_ref=src, dst_ref=dst, send_sem=send, recv_sem=recv, device_id=where, device_id_type=MESH
        )

    def launch(*args):
        copy = remote(*args)
        copy.start()
        return copy

    def tile_copy(where, slot):
        return remote(gath.at[own], gath.at[own], g_send.at[slot], g_recv.at[own], (s, where))

    def tile_wait(slot):
        remote(gath.at[own], gath.at[slot], g_send.at[slot], g_recv.at[slot], (s, t_next)).wait_recv()

    def level_copy(row, where, k):
        part = gath.at[pl.ds(row * columns, columns)]
        return remote(part, part, l_send.at[k], l_recv.at[row], (s, where))

    def halo_copy(side):
        where = (s, t_next if side == UP else t_prev)
        return remote(htile.at[side], hrecv.at[side], h_send.at[side], h_recv.at[side], where)

    def wrap_copy():
        return remote(
            htile.at[DOWN], wrap, h_send.at[DOWN], w_recv, (s, column(columns - 1) * run + h)
        )

    def wrap_on():
        return remote(wrap, hrecv.at[DOWN], w_send, h_recv.at[DOWN], (s, x * run + run - 1))

    halo_copy(UP).start()
    pl.when(z > 0)(lambda: halo_copy(DOWN).start())
    pl.when(z == 0)(lambda: wrap_copy().start())

    for row in range(run):

        @pl.when((z >= h) | (row < h))
        def _():
            for offset in others_x:
                tile_copy(column(offset) * run + row, row * columns + column(offset)).start()
            pl.when(row != z)(lambda: tile_copy(x * run + row, row * columns + x).start())

    @pl.when(lower)
    def _():
        for offset in others_x:
            tile_wait(z * columns + column(offset))
        level_copy(z, t + h, z).start()

    for row in range(h):

        @pl.when(row == z - h)
        def _():
            level_copy(row, t_next, row).wait_recv()
            for k in range(h):
                if k != row:
                    level_copy(row, x * run + h + k, k).start()

    @pl.when(z == h)
    def _():
        wrap_copy().wait_recv()
        wrap_on().start()

    for q in range(6):
        pl.when(heights[q] < level)(functools.partial(answer, q))
    halo_copy(UP).wait_recv()
    halo_copy(DOWN).wait_recv()

    hbuf[...] = jnp.zeros_like(hbuf)

    def set_halo(lo, hi):
        for p in range(2):
            hbuf[p, 0:3, :] = lo[p * 4 : p * 4 + 3, :]
            hbuf[p, 3:6, :] = hi[p * 4 : p * 4 + 3, :]

    def set_velocity(ustar):
        rows = []
        for shift in (0, 1):
            for d in range(3):
                for p in range(2):
                    x = ustar[d][p]
                    rows.append(pltpu.roll(x, 127, 1) if shift else x)
        for shift in (0, 1):
            for p in range(2):
                x = hbuf[p]
                rows.append(pltpu.roll(x, 127, 1) if shift else x)
        vs[...] = split(jnp.concatenate(rows, axis=0), 1)

    set_halo(hrecv[UP], hrecv[DOWN])
    set_velocity(ustar)

    tiles = n_trans // columns
    width = tiles * 128
    rows_of = tiles // columns
    first_row = (t * 8).astype(jnp.float32)

    def return_copy(where, slot):
        return remote(uret.at[slot], urecv.at[own], u_send.at[slot], u_recv.at[own], (s, where))

    def return_wait(slot):
        remote(uret.at[slot], urecv.at[slot], u_send.at[slot], u_recv.at[slot], (s, t_next)).wait_recv()

    def await_tiles(row, offsets):
        for offset in offsets:
            tile_wait(row * columns + column(offset))

    def await_row(row, own_half):
        if own_half:
            pl.when(row != z)(lambda: await_tiles(row, range(columns)))
            pl.when((row == z) & (z >= h))(lambda: await_tiles(row, others_x))
        else:
            pl.when(lower)(lambda: await_tiles(row, range(columns)))
            pl.when((z >= h) & (row != z - h))(lambda: level_copy(row, t_next, 0).wait_recv())

    def marker_pass(step):
        def chunk(j):
            at = j
            if step == 0:
                at = jnp.where(lower, j, columns - 1 - j)
                for k in range(rows_of):
                    await_row(at * rows_of + k, j < columns // 2)
            first = at * tiles
            tile = jnp.concatenate([gath[first + i] for i in range(tiles)], axis=1)
            fx, fy, fz = tile[1:2], tile[2:3], tile[3:4]
            b = jnp.floor(tile[0:1] * (1.0 / 128.0))
            if step == 0:
                e = tile[0:1] - 128.0 * b
                depth = lax.broadcasted_iota(jnp.int32, (128, width), 0).astype(jnp.float32)
                pick = jnp.where(depth == e, 1.0, 0.0).astype(jnp.bfloat16)
                onehot[at] = pick
            else:
                pick = onehot[at]
            r = lax.dot_general(
                vs[...],
                jnp.concatenate([pick, pick], axis=0),
                (((1,), (0,)), ((), ())),
                preferred_element_type=jnp.float32,
            )
            gx, gy, gz = 1.0 - fx, 1.0 - fy, 1.0 - fz
            local = lax.broadcasted_iota(jnp.int32, (8, width), 0).astype(jnp.float32)
            rel = b - first_row
            wy = jnp.where(local == rel, gy, 0.0) + jnp.where(local == rel + 1.0, fy, 0.0)
            wh = jnp.where(
                local < 3.0, jnp.where(rel == -1.0, gy, 0.0), jnp.where(rel == 7.0, fy, 0.0)
            )

            def lerp(at):
                planes = []
                for p in range(2):
                    low, high = at(0, p), at(1, p)
                    planes.append(low * gz + high * fz)
                return planes[0] * gx + planes[1] * fx

            edge = wh * lerp(lambda shift, p: r[(12 + shift * 2 + p) * 8 : (12 + shift * 2 + p) * 8 + 8])
            vel = []
            for d in range(3):
                own = lerp(
                    lambda shift, p: r[((shift * 3 + d) * 2 + p) * 8 : ((shift * 3 + d) * 2 + p) * 8 + 8]
                )
                vel.append(
                    jnp.sum(wy * own, axis=0, keepdims=True) + edge[d : d + 1] + edge[3 + d : 4 + d]
                )
            if step == STEPS - 1:
                mine = (rel >= 0.0) & (rel <= 7.0)
                for d in range(3):
                    back_to = jnp.where(mine, vel[d], 0.0)
                    for i in range(tiles):
                        uret[first + i, d : d + 1, :] = back_to[:, i * 128 : i * 128 + 128]
            spread = []
            wyz = [wy * gz, wy * fz]
            wx = (gx, fx)
            pushes = [tile[7:8] * (tile[4 + d : 5 + d] - vel[d]) for d in range(3)]
            for shift in (0, 1):
                for d in range(3):
                    for p in range(2):
                        spread.append(wyz[shift] * (pushes[d] * wx[p]))
            return lax.dot_general(
                split(jnp.concatenate(spread, axis=0), 0),
                pick,
                (((1,), (1,)), ((), ())),
                preferred_element_type=jnp.float32,
            )

        total = None
        for j in range(columns):
            part = chunk(j)
            total = part if total is None else total + part
        total = total[0:96] + total[96:192]
        g = []
        for d in range(3):
            planes = []
            for p in range(2):
                low = total[(d * 2 + p) * 8 : (d * 2 + p) * 8 + 8]
                high = total[((3 + d) * 2 + p) * 8 : ((3 + d) * 2 + p) * 8 + 8]
                planes.append(low + pltpu.roll(high, 1, 1))
            g.append(jnp.stack(planes))
        return g

    row_of = lax.broadcasted_iota(jnp.int32, (8, 128), 0)

    def deep(post):
        return [
            [
                pltpu.roll(post[i][p], VEL[i][2] % 128, 1) if VEL[i][2] else post[i][p]
                for p in range(2)
            ]
            for i in range(19)
        ]

    def put_row(step, side, at, value):
        if step < STEPS - 1:
            ysend[side, 0, at : at + 1, :] = value
        else:
            ylast[side, at : at + 1, :] = value

    def got_row(step, side, at):
        if step < STEPS - 1:
            return yrecv[side, 0, at : at + 1, :]
        return ylast_recv[side, at : at + 1, :]

    def exchange(step, moved):
        sent = []
        for q, i in enumerate(GO_RIGHT):
            xsend[step, 0, q] = moved[i][1]
        for q, i in enumerate(GO_LEFT):
            xsend[step, 1, q] = moved[i][0]
        sent.append(launch(xsend.at[step, 0], xrecv.at[step, 0], x_send.at[step, 0], x_recv.at[step, 0], (s_next, t)))
        sent.append(launch(xsend.at[step, 1], xrecv.at[step, 1], x_send.at[step, 1], x_recv.at[step, 1], (s_prev, t)))
        for q, (i, source, unused) in enumerate(ROWS_UP):
            put_row(step, UP, q, moved[i][source][7:8])
        for q, (i, source, unused) in enumerate(ROWS_DOWN):
            put_row(step, DOWN, q, moved[i][source][0:1])
        corner = ((7, 1, 7), (10, 0, 7), (9, 1, 0), (8, 0, 0))
        for q, (i, source, row) in enumerate(corner):
            dsend[step, q] = jnp.broadcast_to(moved[i][source][row : row + 1], (8, 128))
        if step < STEPS - 1:
            for side, sign, row in ((UP, 1, 7), (DOWN, -1, 0)):
                inner = row - sign
                for p in range(2):
                    level = {0: [], sign: []}
                    own = []
                    for i in range(19):
                        source = p - VEL[i][0]
                        if source not in (0, 1):
                            continue
                        if VEL[i][1] in level:
                            level[VEL[i][1]].append((i, moved[i][source]))
                        else:
                            own.append((i, moved[i][source]))
                    for m in range(4):
                        flat = sum_moment(level[0], m)
                        steep = sum_moment(level[sign], m)
                        value = 0.0
                        if flat is not None:
                            value = flat[row : row + 1]
                        if steep is not None:
                            value = value + steep[inner : inner + 1]
                        ysend[side, 1, p * 4 + m : p * 4 + m + 1, :] = value
                        mine = sum_moment(own, m)
                        mown[side, p * 4 + m : p * 4 + m + 1, :] = (
                            jnp.zeros((1, 128), jnp.float32) if mine is None else mine[7 - row : 8 - row]
                        )
                for q, names, source, at in ((0, GO_RIGHT, 1, 0), (1, GO_LEFT, 0, 4)):
                    q = q + (0 if side == UP else 2)
                    flat_set = [(i, moved[i][source]) for i in names if VEL[i][1] == 0]
                    steep_set = [(i, moved[i][source]) for i in names if VEL[i][1] == sign]
                    for m in range(4):
                        flat = sum_moment(flat_set, m)
                        steep = sum_moment(steep_set, m)
                        value = 0.0
                        if flat is not None:
                            value = flat[row : row + 1]
                        if steep is not None:
                            value = value + steep[inner : inner + 1]
                        dsend[step, q, at + m : at + m + 1, :] = value
        for q, where in enumerate(diagonals):
            sent.append(launch(dsend.at[step, q], drecv.at[step, q], d_send.at[step, q], d_recv.at[step, q], where))
        for side, where in ((UP, (s, t_next)), (DOWN, (s, t_prev))):
            if step < STEPS - 1:
                source, target = ysend.at[side], yrecv.at[side]
            else:
                source, target = ylast.at[side], ylast_recv.at[side]
            sent.append(launch(source, target, y_send.at[step, side], y_recv.at[step, side], where))
        return sent

    def sum_moment(members, m):
        if m == 0:
            return add_up((1, value) for i, value in members)
        return add_up((VEL[i][m - 1], value) for i, value in members)

    def stream(step, moved):
        new = []
        for i in range(19):
            cx, cy, unused = VEL[i]
            planes = []
            for p in range(2):
                source = p - cx
                if source in (0, 1):
                    tile = moved[i][source]
                elif cx == 1:
                    tile = xrecv[step, 0, GO_RIGHT.index(i)]
                else:
                    tile = xrecv[step, 1, GO_LEFT.index(i)]
                if cy != 0:
                    side = UP if cy == 1 else DOWN
                    rows = ROWS_UP if cy == 1 else ROWS_DOWN
                    if source in (0, 1):
                        at = rows.index((i, source, p))
                        edge = got_row(step, side, at)
                    else:
                        q = (0 if cx == 1 else 1) + (0 if cy == 1 else 2)
                        at = 4 if cx == 1 else 0
                        edge = drecv[step, q, at : at + 1, :]
                    tile = jnp.where(row_of == (0 if cy == 1 else 7), edge, pltpu.roll(tile, cy % 8, 0))
                planes.append(tile)
            new.append(jnp.stack(planes))
        return new

    def edge_moments(step, side):
        low = row_of < 4
        total = yrecv[side, 1] + mown[side]
        q = 0 if side == UP else 2
        total = total + jnp.where(low, drecv[step, q], drecv[step, q + 1])
        sign = 1 if side == UP else -1
        row = 0 if side == UP else 7
        i = 9 if side == UP else 7
        left = xrecv[step, 0, GO_RIGHT.index(i), row : row + 1, :]
        i = 8 if side == UP else 10
        right = xrecv[step, 1, GO_LEFT.index(i), row : row + 1, :]
        total = total + jnp.where((row_of == 0) | (row_of == 1), left, 0.0)
        total = total + jnp.where(row_of == 2, -sign * left, 0.0)
        total = total + jnp.where(row_of == 4, right, 0.0)
        total = total + jnp.where(row_of == 5, -right, 0.0)
        total = total + jnp.where(row_of == 6, -sign * right, 0.0)
        return total

    def edge_velocity(total):
        values = []
        for p in range(2):
            inv = 1.0 / total[p * 4 : p * 4 + 1]
            values.append(total[p * 4 + 1 : p * 4 + 4] * inv)
        return values

    solid = solid_ref[...]

    def others(action):
        for row in range(run):
            for offset in others_x:
                action(row * columns + column(offset))
            pl.when(row != z)(functools.partial(action, row * columns + x))

    def finish_gather():
        halo_copy(UP).wait_send()
        halo_copy(DOWN).wait_send()
        pl.when(z == h)(lambda: wrap_on().wait_send())
        for row in range(run):

            @pl.when((z >= h) | (row < h))
            def _():
                for offset in others_x:
                    tile_copy(t_next, row * columns + column(offset)).wait_send()
                pl.when(row != z)(lambda: tile_copy(t_next, row * columns + x).wait_send())

        pl.when(lower)(lambda: level_copy(z, t_next, z).wait_send())
        for k in range(h):
            pl.when((z >= h) & (k != z - h))(lambda: level_copy(0, t_next, k).wait_send())

    g = marker_pass(0)
    moved = deep(collide(f, rho, mom, g, solid))
    for q in range(6):
        pl.when(heights[q] > level)(functools.partial(await_ready, q))
    first_rims = exchange(0, moved)
    finish_gather()
    for copy in first_rims:
        copy.wait_recv()
    f = stream(0, moved)
    low = edge_velocity(edge_moments(0, UP))
    high = edge_velocity(edge_moments(0, DOWN))
    for p in range(2):
        hbuf[p, 0:3, :] = low[p]
        hbuf[p, 3:6, :] = high[p]
    rho, mom = moments(f)
    inv = 1.0 / rho
    set_velocity([mom[d] * inv for d in range(3)])

    g = marker_pass(1)

    moved = deep(collide(f, rho, mom, g, solid))
    rims = exchange(1, moved)
    for row in range(run):
        for offset in others_x:
            return_copy(column(offset) * run + row, row * columns + column(offset)).start()
        pl.when(row != z)(lambda: return_copy(x * run + row, row * columns + x).start())
    urecv[own] = uret[own]
    others(return_wait)
    vel = [urecv[k] for k in range(n_trans)]
    while len(vel) > 1:
        vel = [vel[k] + vel[k + 1] for k in range(0, len(vel), 2)]
    force_ref[...] = gath[own, 7:8, :] * (gath[own, 4:7, :] - vel[0][0:3])
    for copy in first_rims:
        copy.wait_send()
    others(lambda slot: return_copy(t_next, slot).wait_send())
    for copy in rims:
        copy.wait_recv()
    f = stream(1, moved)
    for i in range(19):
        out_ref[i] = f[i]
    for copy in rims:
        copy.wait_send()


def per_device(n_stream, n_trans, populations, solid, support, fractions, target, area):
    columns = 4 if n_trans % 32 == 0 else 2
    run = n_trans // columns
    dma = pltpu.SemaphoreType.DMA
    f32 = jnp.float32
    vmem = pl.BlockSpec(memory_space=pltpu.VMEM)
    markers = support.shape[0]
    return pl.pallas_call(
        functools.partial(kernel, n_stream, n_trans, columns),
        out_shape=(
            jax.ShapeDtypeStruct(populations.shape, f32),
            jax.ShapeDtypeStruct((3, markers), f32),
        ),
        in_specs=[pl.BlockSpec(memory_space=pltpu.MemorySpace.HBM)] * 6,
        out_specs=(vmem, vmem),
        scratch_shapes=[
            pltpu.VMEM(populations.shape, f32),
            pltpu.VMEM(solid.shape, jnp.int32),
            pltpu.VMEM((1, markers), jnp.int32),
            pltpu.VMEM((3, markers), f32),
            pltpu.VMEM((3, markers), f32),
            pltpu.VMEM((1, markers), f32),
            pltpu.VMEM((n_trans, 8, 128), f32),
            pltpu.VMEM((columns, 128, run * 128), jnp.bfloat16),
            pltpu.VMEM((128, 256), jnp.bfloat16),
            pltpu.VMEM((2, 8, 128), f32),
            pltpu.VMEM((2, 8, 128), f32),
            pltpu.VMEM((8, 128), f32),
            pltpu.VMEM((2, 8, 128), f32),
            pltpu.VMEM((2, 2, 5, 8, 128), f32),
            pltpu.VMEM((2, 2, 5, 8, 128), f32),
            pltpu.VMEM((2, 2, 8, 128), f32),
            pltpu.VMEM((2, 2, 8, 128), f32),
            pltpu.VMEM((2, 8, 128), f32),
            pltpu.VMEM((2, 8, 128), f32),
            pltpu.VMEM((2, 8, 128), f32),
            pltpu.VMEM((2, 4, 8, 128), f32),
            pltpu.VMEM((2, 4, 8, 128), f32),
            pltpu.VMEM((n_trans, 3, 128), f32),
            pltpu.VMEM((n_trans, 3, 128), f32),
            dma((6,)),
            pltpu.SemaphoreType.REGULAR((8,)),
            dma,
            dma,
            dma((run,)),
            dma((run,)),
            dma((n_trans,)),
            dma((n_trans,)),
            dma((2,)),
            dma((2,)),
            dma((2, 2)),
            dma((2, 2)),
            dma((2, 2)),
            dma((2, 2)),
            dma((2, 4)),
            dma((2, 4)),
            dma((n_trans,)),
            dma((n_trans,)),
        ],
        compiler_params=pltpu.CompilerParams(
            collective_id=0, has_side_effects=True, vmem_limit_bytes=56 * 1024 * 1024
        ),
        name="tract",
    )(
        populations,
        solid,
        support.reshape(1, markers),
        fractions,
        target,
        area.reshape(1, markers),
    )


def solution(mesh):
    placed = (
        P(None, "stream", "trans", None),
        P("stream", "trans", None),
        P(("stream", "trans")),
        P(None, ("stream", "trans")),
        P(None, ("stream", "trans")),
        P(("stream", "trans")),
    )
    return jax.shard_map(
        functools.partial(per_device, mesh.shape["stream"], mesh.shape["trans"]),
        mesh=mesh,
        in_specs=placed,
        out_specs=(P(None, "stream", "trans", None), P(None, ("stream", "trans"))),
        check_vma=False,
    )
```
